128 devices in a mesh: section: 2 (over core), lat: 8 (over z_lo, x), lon: 8 (over z_hi, y).
Axes of the slice: x: 4, y: 4, z: 4 (z_hi: 2, z_lo: 2; z = z_hi * 2 + z_lo), core: 2. Of those that a mesh axis runs over, the one named last changes fastest.
Arguments:
- level_tokens: bfloat16 [1, 8, 8, 8, 24, 13, 512], P(None, None, 'lat', None, 'lon'), may hold values from -6 to 6
- enc_query: bfloat16 [3, 512], replicated, may hold values from -6 to 6
- encoder_projection_weights: bfloat16 [4, 512, 512], replicated, may hold values from -0.25 to 0.25
- attn_proj: bfloat16 [2, 4, 512, 512], replicated, may hold values from -0.25 to 0.25
- expand_matrix_pair: bfloat16 [2, 512, 2048], replicated, may hold values from -0.25 to 0.25
- contract_matrix_pair: bfloat16 [2, 2048, 512], replicated, may hold values from -0.125 to 0.125
- normalization_gain_table: float32 [2, 2, 512], replicated, may hold values from 0.25 to 1.75
Outputs:
- predicted_latents: bfloat16 [1, 64, 192, 3, 512], P(None, 'lat', 'lon', None, 'section')
The draws below stay inside these ranges and needn't reach their ends.
All inputs are finite; a program needn't handle non-finite values.
Results may differ from the reference program's by a relative error of at most 0.023.
Values may be sent and summed in bfloat16 or wider, within the bound.
No kernel may reach another device: no remote copies, remote signals or barrier semaphores. Data moves between devices by JAX's collectives and lax.ppermute only.
A program may use at most 128 MiB of HBM per device.

```python
import jax
import jax.numpy as jnp
from jax import lax

D = 512
FF = 2048
HEADS = 16
C = 13
L = 3
WIN_LAT = 4
WIN_LON = 12
M = 1
TH = 8
TW = 24
SHIFT_LAT = 2
SHIFT_LON = 6
NLAT = 64
NLON = 192
N_LAT = 8
N_LON = 8


def shard_levels(own_key, extent, cuts, smallest, high):
    def one(dim, shards_of):
        heights = jax.random.uniform(jax.random.fold_in(jax.random.fold_in(own_key, 6), dim), (shards_of,), jnp.float32, smallest / len(cuts), high / len(cuts))
        return jnp.repeat(jnp.exp(heights), extent[dim] // shards_of).reshape((-1,) + (1,) * (len(extent) - dim - 1))

    gain = one(*cuts[0])
    for cut in cuts[1:]:
        gain = gain * one(*cut)
    return gain


def scatter_about(rng, dims, width, reach, shards=(), held_as=jnp.bfloat16):
    factor_of = shard_levels(rng, dims, shards, -0.22, 0.18) if shards else 1.0
    result = jax.random.normal(rng, dims, jnp.float32) * width * factor_of
    return jnp.minimum(jnp.maximum(result, -reach), reach).astype(held_as)


def setup_inputs(seed: int = 0) -> dict:
    key_of = jax.random.split(jax.random.key(seed), 8)
    level_tokens = scatter_about(key_of[0], (M, N_LAT, TH, N_LON, TW, C, D), 1.0, 6.0, ((2, 8), (4, 8)))
    enc_query = scatter_about(key_of[1], (L, D), 1.0, 6.0)
    encoder_projection_weights = scatter_about(key_of[2], (4, D, D), D ** -0.5, 0.25)
    attn_proj = scatter_about(key_of[3], (2, 4, D, D), D ** -0.5, 0.25)
    expand_matrix_pair = scatter_about(key_of[4], (2, D, FF), D ** -0.5, 0.25)
    contract_matrix_pair = scatter_about(key_of[5], (2, FF, D), FF ** -0.5, 0.125)
    normalization_gain_table = jnp.clip(1.0 + 0.15 * jax.random.normal(key_of[6], (2, 2, D), jnp.float32), 0.25, 1.75)
    return dict(level_tokens=level_tokens, enc_query=enc_query, encoder_projection_weights=encoder_projection_weights, attn_proj=attn_proj, expand_matrix_pair=expand_matrix_pair, contract_matrix_pair=contract_matrix_pair, normalization_gain_table=normalization_gain_table)


EPS = 1e-05
NEG_FILL = -1e+30

def normed(values, gain_row):
    values = values.astype(jnp.float32)
    center = values - lax.optimization_barrier(jnp.mean(values, -1, keepdims=True))
    spread = lax.optimization_barrier(jnp.mean(center * center, -1, keepdims=True))
    return center * lax.rsqrt(spread + EPS) * gain_row.astype(jnp.float32)

def encode_levels(patch_levels, enc_query, encoder_projection_weights):
    model_width = patch_levels.shape[-1]
    level_count = patch_levels.shape[-2]
    latent_count = enc_query.shape[0]
    head_size = model_width // HEADS
    flat_levels = patch_levels.reshape(-1, model_width)
    patch_count = flat_levels.shape[0] // level_count
    queries = jnp.dot(enc_query, encoder_projection_weights[0], preferred_element_type=jnp.float32).astype(jnp.bfloat16)
    key_all = jnp.dot(flat_levels, encoder_projection_weights[1], preferred_element_type=jnp.float32).astype(jnp.bfloat16)
    value_all = jnp.dot(flat_levels, encoder_projection_weights[2], preferred_element_type=jnp.float32).astype(jnp.bfloat16)
    key_all = key_all.reshape(patch_count, level_count, HEADS, head_size)
    value_all = value_all.reshape(patch_count, level_count, HEADS, head_size)
    latent = queries.reshape(latent_count, HEADS, head_size)
    scores = jnp.einsum('lhe,pche->phlc', latent.astype(jnp.float32), key_all.astype(jnp.float32)) * head_size ** (-0.5)
    weights = jax.nn.softmax(scores, axis=-1).astype(jnp.bfloat16)
    mixed = jnp.einsum('phlc,pche->plhe', weights.astype(jnp.float32), value_all.astype(jnp.float32)).astype(jnp.bfloat16)
    projected = jnp.dot(mixed.reshape(-1, model_width), encoder_projection_weights[3], preferred_element_type=jnp.float32)
    projected = projected.reshape(patch_count, latent_count, model_width)
    encoded = (enc_query.astype(jnp.float32)[None] + projected).astype(jnp.bfloat16)
    return encoded.reshape(patch_levels.shape[:-2] + (latent_count, model_width))

def to_windows(blocks):
    grid_rows, grid_cols, level_count, last = blocks.shape
    blocks = blocks.reshape(grid_rows // WIN_LAT, WIN_LAT, grid_cols // WIN_LON, WIN_LON, level_count, last)
    blocks = blocks.transpose(0, 2, 1, 3, 4, 5)
    return blocks.reshape(-1, WIN_LAT * WIN_LON * level_count, last)

def from_windows(blocks, grid_rows, grid_cols, level_count):
    last = blocks.shape[-1]
    blocks = blocks.reshape(grid_rows // WIN_LAT, grid_cols // WIN_LON, WIN_LAT, WIN_LON, level_count, last)
    blocks = blocks.transpose(0, 2, 1, 3, 4, 5)
    return blocks.reshape(grid_rows, grid_cols, level_count, last)

def window_attention(tokens, proj, gain_row, labels):
    grid_rows, grid_cols, level_count, model_width = tokens.shape
    head_size = model_width // HEADS
    flat_in = normed(tokens, gain_row).astype(jnp.bfloat16).reshape(-1, model_width)
    parts = []
    for index in range(3):
        part = jnp.dot(flat_in, proj[index], preferred_element_type=jnp.float32).astype(jnp.bfloat16)
        part = to_windows(part.reshape(grid_rows, grid_cols, level_count, model_width))
        parts.append(part.reshape(part.shape[0], part.shape[1], HEADS, head_size).astype(jnp.float32))
    scores = jnp.einsum('wqhe,wkhe->whqk', parts[0], parts[1]) * head_size ** (-0.5)
    if labels is not None:
        spread_labels = jnp.broadcast_to(labels[:, :, None, None], (grid_rows, grid_cols, level_count, 1))
        window_lab = to_windows(spread_labels)[..., 0]
        same = window_lab[:, :, None] == window_lab[:, None, :]
        scores = jnp.where(same[:, None], scores, NEG_FILL)
    weights = jax.nn.softmax(scores, axis=-1).astype(jnp.bfloat16)
    mixed = jnp.einsum('whqk,wkhe->wqhe', weights.astype(jnp.float32), parts[2]).astype(jnp.bfloat16)
    mixed = from_windows(mixed.reshape(mixed.shape[0], mixed.shape[1], model_width), grid_rows, grid_cols, level_count)
    out_flat = jnp.dot(mixed.reshape(-1, model_width), proj[3], preferred_element_type=jnp.float32).astype(jnp.bfloat16)
    return out_flat.reshape(tokens.shape)

def dense_sublayer_apply(tokens, gain_row, w_in, w_out):
    model_width = tokens.shape[-1]
    flat_in = normed(tokens, gain_row).astype(jnp.bfloat16).reshape(-1, model_width)
    hidden = jax.nn.gelu(jnp.dot(flat_in, w_in, preferred_element_type=jnp.float32), approximate=False).astype(jnp.bfloat16)
    return jnp.dot(hidden, w_out, preferred_element_type=jnp.float32).reshape(tokens.shape)

def reference(level_tokens, enc_query, encoder_projection_weights, attn_proj, expand_matrix_pair, contract_matrix_pair, normalization_gain_table):
    row_labels = (jnp.arange(NLAT, dtype=jnp.int32) >= NLAT - SHIFT_LAT).astype(jnp.int32)
    labels = jnp.broadcast_to(row_labels[:, None], (NLAT, NLON))
    ensemble_results = []
    for member in range(M):
        grid = level_tokens[member].reshape(NLAT, NLON, C, D)
        encoded = encode_levels(grid, enc_query, encoder_projection_weights)
        attended = window_attention(encoded, attn_proj[0], normalization_gain_table[0, 0], None)
        first_mid = (encoded.astype(jnp.float32) + attended.astype(jnp.float32)).astype(jnp.bfloat16)
        first_out = (first_mid.astype(jnp.float32) + dense_sublayer_apply(first_mid, normalization_gain_table[0, 1], expand_matrix_pair[0], contract_matrix_pair[0])).astype(jnp.bfloat16)
        shifted = jnp.roll(first_out, (-SHIFT_LAT, -SHIFT_LON), (0, 1))
        shifted_attn = window_attention(shifted, attn_proj[1], normalization_gain_table[1, 0], labels)
        back = jnp.roll(shifted_attn, (SHIFT_LAT, SHIFT_LON), (0, 1))
        later_hidden_state = (first_out.astype(jnp.float32) + back.astype(jnp.float32)).astype(jnp.bfloat16)
        predicted_latents = (later_hidden_state.astype(jnp.float32) + dense_sublayer_apply(later_hidden_state, normalization_gain_table[1, 1], expand_matrix_pair[1], contract_matrix_pair[1])).astype(jnp.bfloat16)
        ensemble_results.append(predicted_latents)
    return jnp.stack(ensemble_results)
```

```python
import math

import jax
import jax.numpy as jnp
import numpy as np
from jax import lax
from jax.experimental import pallas as pl
from jax.experimental.pallas import tpu as pltpu
from jax.sharding import PartitionSpec as P

F32 = jnp.float32
BF16 = jnp.bfloat16
EPS = 1e-05
NEG = -1e30
HEADS = 16
HEAD = 32
GROUP = 8
LEVELS = 13
LATENTS = 3
D = 512
HALF = 256
FF = 2048
TOKENS = 144
QUAD = 36
CHUNK = 24
SCALE = math.log2(math.e) / math.sqrt(HEAD)
ALL_AXES = ("section", "lat", "lon")
VMEM_LIMIT = 56 * 1024 * 1024


def one_hot(rows, cols, pairs):
    out = np.zeros((rows, cols), np.float32)
    for row, col in pairs:
        out[row, col] = 1.0
    return out


def encoder_tables():
    cells = 24
    gather = one_hot(
        LEVELS * cells, 16 * cells,
        [(c * cells + i, i * 16 + c) for c in range(LEVELS) for i in range(cells)],
    )
    scatter = [
        one_hot(
            8 * CHUNK, LATENTS * cells,
            [
                (b * CHUNK + half * 9 + w * 3 + l, l * cells + b * 3 + w)
                for b in range(8) for w in range(3) for l in range(3)
            ],
        )
        for half in range(2)
    ]
    return gather, np.stack(scatter)


def compact_table():
    tables = []
    for half in range(2):
        pairs = []
        for rh in range(2):
            for ch in range(2):
                for r in range(2):
                    for c in range(6):
                        for l in range(3):
                            token = ((rh * 2 + ch) * 2 + r) * 18 + c * 3 + l
                            col = ch * 6 + c
                            chunk = (2 * rh + r) * 4 + col // 3
                            pairs.append((token, chunk * CHUNK + half * 9 + (col % 3) * 3 + l))
        tables.append(one_hot(TOKENS, 16 * CHUNK, pairs))
    return np.stack(tables)


def run(dst, src):
    return [(dst + i, src + i) for i in range(QUAD)]


def shifted_tables():
    source = np.stack([
        one_hot(144, 288, run(36, 0) + run(108, 144)),
        one_hot(144, 288, run(0, 36) + run(36, 72) + run(72, 180) + run(108, 216)),
        one_hot(144, 288, run(0, 108) + run(72, 252)),
    ])
    left = np.stack([
        one_hot(144, 144, run(0, 0) + run(72, 36)),
        one_hot(144, 144, run(0, 108) + run(72, 72)),
    ])
    right = np.stack([
        one_hot(144, 144, run(36, 0) + run(108, 36)),
        one_hot(144, 144, run(36, 108) + run(108, 72)),
    ])
    queries = one_hot(160, 144, run(0, 0) + run(40, 36) + run(76, 72) + run(112, 108))
    rowmajor = one_hot(
        144, 144,
        [
            (r * 72 + (cb * 6 + c) * 3 + l, cb * 36 + r * 18 + c * 3 + l)
            for cb in range(4) for r in range(2) for c in range(6) for l in range(3)
        ],
    )
    back = rowmajor @ queries.T
    return source, left, right, queries, back, rowmajor


def ones_table():
    out = np.zeros((1152, 256), np.float32)
    for h in range(GROUP):
        out[h * 128 : (h + 1) * 128, h * HEAD : (h + 1) * HEAD] = 1.0
        out[1024 + h * 16 : 1024 + (h + 1) * 16, h * HEAD : (h + 1) * HEAD] = 1.0
    return out


def dot(a, b):
    return jnp.dot(a, b, preferred_element_type=F32)


def pick(table, rows):
    return dot(table, rows).astype(BF16)


def normed(values, gain):
    center = values - jnp.mean(values, -1, keepdims=True)
    spread = jnp.mean(center * center, -1, keepdims=True)
    return (center * lax.rsqrt(spread + EPS) * gain).astype(BF16)


def gelu(x):
    return 0.5 * x * (1.0 + lax.erf(x * (1.0 / math.sqrt(2.0))))


def by_head(block):
    lane = lax.broadcasted_iota(jnp.int32, (1, HALF), 1) // HEAD
    main, rest = block[:128], block[128:]
    zero = jnp.zeros((), block.dtype)
    parts = [jnp.where(lane == h, main, zero) for h in range(GROUP)]
    parts += [jnp.where(lane == h, rest, zero) for h in range(GROUP)]
    return jnp.concatenate(parts, axis=0)


def attend(q, k, v, bias, ones):
    outs = []
    lane = lax.broadcasted_iota(jnp.int32, (1, 128), 1) // 16
    for g in range(HEADS // GROUP):
        cols = slice(g * HALF, (g + 1) * HALF)
        scores = lax.dot_general(
            q[:, cols], by_head(k[:, cols]), (((1,), (1,)), ((), ())),
            preferred_element_type=F32,
        )
        if bias is not None:
            scores = scores + bias
        tail = scores[:, 1024:]
        shift = jnp.zeros_like(tail)
        parts = []
        for h in range(GROUP):
            own = scores[:, h * 128 : (h + 1) * 128]
            top = jnp.max(
                jnp.maximum(own, jnp.where(lane == h, tail, -jnp.inf)), axis=-1, keepdims=True
            )
            parts.append(jnp.exp2(own - top).astype(BF16))
            shift = jnp.where(lane == h, top, shift)
        parts.append(jnp.exp2(tail - shift).astype(BF16))
        weights = jnp.concatenate(parts, axis=1)
        outs.append(dot(weights, by_head(v[:, cols])) / dot(weights, ones))
    return jnp.concatenate(outs, axis=1)


def feed_forward(tokens, w_in, w_out):
    total = None
    step = 512
    for i in range(FF // step):
        cols = slice(i * step, (i + 1) * step)
        hidden = gelu(dot(tokens, w_in[:, cols])).astype(BF16)
        part = dot(hidden, w_out[cols, :])
        total = part if total is None else total + part
    return total


def encode_kernel(x_ref, query_ref, w_ref, gather_ref, scatter_ref, out_ref, rows, weights):
    section = lax.axis_index("section")
    half = pl.ds(pl.multiple_of(section * HALF, HALF), HALF)

    @pl.when(pl.program_id(0) == 0)
    def _():
        rows[...] = jnp.zeros_like(rows)
        query = jnp.concatenate([query_ref[...], jnp.zeros((5, D), BF16)], axis=0)
        latent = dot(query, w_ref[0, :, half]).astype(BF16).astype(F32)
        turned = latent.T
        keys = w_ref[1, :, half]
        weights[:, :HALF] = w_ref[2, :, half]
        same = (
            lax.broadcasted_iota(jnp.int32, (HALF, HALF), 0) // HEAD
            == lax.broadcasted_iota(jnp.int32, (HALF, HALF), 1) // HEAD
        )
        for l in range(LATENTS):
            spread = jnp.where(same, turned[:, l : l + 1], 0.0).astype(BF16)
            weights[:, HALF * (l + 1) : HALF * (l + 2)] = (dot(keys, spread) * SCALE).astype(BF16)

    for i in range(24):
        rows[16 * i : 16 * i + LEVELS, :] = x_ref[i]
    tokens = pick(gather_ref[...], rows[...])
    mixed = []
    value = dot(tokens, weights[:, :HALF]).reshape(LEVELS, 24, HALF)
    for l in range(LATENTS):
        scores = dot(tokens, weights[:, HALF * (l + 1) : HALF * (l + 2)])
        scores = scores.reshape(LEVELS, 24, HALF)
        expd = jnp.exp2(scores - jnp.max(scores, axis=0, keepdims=True))
        mixed.append(jnp.sum(expd * value, axis=0) / jnp.sum(expd, axis=0))
    mixed = jnp.concatenate(mixed, axis=0).astype(BF16)
    out_ref[...] = (
        dot(scatter_ref[0], mixed[:, :128]) + dot(scatter_ref[1], mixed[:, 128:])
    ).astype(BF16)


def encode(level_tokens, enc_query, weights):
    cells = level_tokens.shape[1] * level_tokens.shape[3] * level_tokens.shape[4]
    source = level_tokens.reshape(cells, LEVELS, D)
    gather, scatter = encoder_tables()
    steps = cells // 24
    return pl.pallas_call(
        encode_kernel,
        grid=(steps,),
        out_shape=jax.ShapeDtypeStruct((steps * 8 * CHUNK, 128), BF16),
        in_specs=[
            pl.BlockSpec((24, LEVELS, D), lambda i: (i, 0, 0)),
            pl.BlockSpec((LATENTS, D), lambda i: (0, 0)),
            pl.BlockSpec((3, D, D), lambda i: (0, 0, 0)),
            pl.BlockSpec(gather.shape, lambda i: (0, 0)),
            pl.BlockSpec(scatter.shape, lambda i: (0, 0, 0)),
        ],
        out_specs=pl.BlockSpec((8 * CHUNK, 128), lambda i: (i, 0)),
        scratch_shapes=[pltpu.VMEM((24 * 16, D), BF16), pltpu.VMEM((D, 4 * HALF), BF16)],
        compiler_params=pltpu.CompilerParams(vmem_limit_bytes=VMEM_LIMIT),
        name="encode_levels",
    )(source, enc_query, weights, jnp.asarray(gather, BF16), jnp.asarray(scatter, BF16))


def first_kernel(
    own_ref, other_ref, query_ref, gain_ref, compact_ref, ones_ref,
    enc_hbm, proj_hbm, in_hbm, out_hbm, x_ref, enc_w, proj, w_in, w_out, sems,
):
    section = lax.axis_index("section")
    copies = [
        pltpu.make_async_copy(enc_hbm.at[3], enc_w, sems.at[0]),
        pltpu.make_async_copy(proj_hbm.at[0], proj, sems.at[1]),
        pltpu.make_async_copy(in_hbm.at[0], w_in, sems.at[2]),
        pltpu.make_async_copy(out_hbm.at[0], w_out, sems.at[3]),
    ]
    for copy in copies:
        copy.start()

    def gathered(ref):
        out = []
        for w in range(2):
            parts = []
            for r in range(4):
                start = pl.multiple_of((section * 4 + r) * 8 * CHUNK + w * 4 * CHUNK, 32)
                parts.append(ref[pl.ds(start, 4 * CHUNK), :])
            block = jnp.concatenate(parts, axis=0)
            out.append(
                jnp.concatenate(
                    [dot(compact_ref[0], block), dot(compact_ref[1], block)], axis=1
                ).astype(BF16)
            )
        return jnp.concatenate(out, axis=0)

    own, other = gathered(own_ref), gathered(other_ref)
    latent = lax.broadcasted_iota(jnp.int32, (2 * TOKENS, 1), 0) % LATENTS
    query = query_ref[...].astype(F32)
    base = jnp.where(
        latent == 0, query[0:1], jnp.where(latent == 1, query[1:2], query[2:3])
    )
    copies[0].wait()
    mine = pl.ds(pl.multiple_of(section * HALF, HALF), HALF)
    theirs = pl.ds(pl.multiple_of((1 - section) * HALF, HALF), HALF)
    tokens = base + dot(own, enc_w[mine, :]) + dot(other, enc_w[theirs, :])
    tokens = tokens.astype(BF16).astype(F32)
    flat = normed(tokens, gain_ref[0, 0:1, :])
    copies[1].wait()
    q = (dot(flat, proj[0]) * SCALE).astype(BF16)
    k = dot(flat, proj[1]).astype(BF16)
    v = dot(flat, proj[2]).astype(BF16)
    mixed = []
    for w in range(2):
        part = slice(w * TOKENS, (w + 1) * TOKENS)
        mixed.append(attend(q[part], k[part], v[part], None, ones_ref[...]))
    mixed = jnp.concatenate(mixed, axis=0).astype(BF16)
    middle = (tokens + dot(mixed, proj[3]).astype(BF16).astype(F32)).astype(BF16).astype(F32)
    flat = normed(middle, gain_ref[0, 1:2, :])
    copies[2].wait()
    copies[3].wait()
    done = middle + feed_forward(flat, w_in, w_out)
    done = jnp.concatenate([done[0:72], done[144:216], done[72:144], done[216:288]], axis=0)
    x_ref[...] = done.astype(BF16)


def vmem():
    return pl.BlockSpec(memory_space=pltpu.VMEM)


def hbm():
    return pl.BlockSpec(memory_space=pl.ANY)


def first_layer(own, other, enc_query, gains, enc_w, proj, w_in, w_out):
    return pl.pallas_call(
        first_kernel,
        out_shape=jax.ShapeDtypeStruct((2 * TOKENS, D), BF16),
        in_specs=[vmem()] * 6 + [hbm()] * 4,
        out_specs=vmem(),
        scratch_shapes=[
            pltpu.VMEM((D, D), BF16),
            pltpu.VMEM((4, D, D), BF16),
            pltpu.VMEM((D, FF), BF16),
            pltpu.VMEM((FF, D), BF16),
            pltpu.SemaphoreType.DMA((4,)),
        ],
        compiler_params=pltpu.CompilerParams(vmem_limit_bytes=VMEM_LIMIT),
        name="first_layer",
    )(
        own, other, enc_query, gains,
        jnp.asarray(compact_table(), BF16), jnp.asarray(ones_table(), BF16),
        enc_w, proj, w_in, w_out,
    )


def second_kernel(
    above_ref, x_ref, below_ref, left_ref, right_ref, gain_ref,
    source_ref, pleft_ref, pright_ref, queries_ref, back_ref, rowmajor_ref, ones_ref,
    proj_hbm, in_hbm, out_hbm, keep_ref, send_ref, proj, w_in, w_out, sems,
):
    section = lax.axis_index("section")
    lat = lax.axis_index("lat")
    copies = [
        pltpu.make_async_copy(proj_hbm.at[1], proj, sems.at[0]),
        pltpu.make_async_copy(in_hbm.at[1], w_in, sems.at[1]),
        pltpu.make_async_copy(out_hbm.at[1], w_out, sems.at[2]),
    ]
    for copy in copies:
        copy.start()
    gain = gain_ref[1, 0:1, :]
    outer = [normed(ref[...].astype(F32), gain) for ref in (above_ref, below_ref)]
    own = normed(x_ref[...].astype(F32), gain)
    own = [own[:TOKENS], own[TOKENS:]]
    left = normed(left_ref[...].astype(F32), gain)
    right = normed(right_ref[...].astype(F32), gain)
    keys, asks = [], []
    for r in range(2):
        block = jnp.concatenate([outer[r], own[r]], axis=0)
        keys.append((dot(source_ref[0], block) + dot(pleft_ref[r], left)).astype(BF16))
        keys.append(pick(source_ref[1], block))
        keys.append((dot(source_ref[2], block) + dot(pright_ref[r], right)).astype(BF16))
        asks.append(pick(queries_ref[...], own[r]))
    keys = jnp.concatenate(keys, axis=0)
    asks = jnp.concatenate(asks, axis=0)
    copies[0].wait()
    q = dot(asks, proj[0]) * SCALE
    k = dot(keys, proj[1]).astype(BF16)
    v = dot(keys, proj[2]).astype(BF16)
    lane = lax.broadcasted_iota(jnp.int32, (1, 1152), 1)
    outside = (lane < 1024) & (lane % 128 < TOKENS // 2)
    edge = [(lat == 0) & (section == 0), (lat == lax.axis_size("lat") - 1) & (section == 1)]
    mixed = []
    for r in range(2):
        bias = jnp.where(outside & edge[r], NEG, 0.0)
        parts = []
        for c, (start, size) in enumerate(((0, 40), (40, 72), (112, 40))):
            part = slice((3 * r + c) * TOKENS, (3 * r + c + 1) * TOKENS)
            asked = q[r * 160 + start : r * 160 + start + size].astype(BF16)
            parts.append(attend(asked, k[part], v[part], bias, ones_ref[...]))
        parts.append(jnp.zeros((8, D), F32))
        mixed.append(pick(back_ref[...], jnp.concatenate(parts, axis=0).astype(BF16)))
    mixed = jnp.concatenate(mixed, axis=0)
    before = jnp.concatenate(
        [dot(rowmajor_ref[...], x_ref[r * TOKENS : (r + 1) * TOKENS, :]) for r in range(2)], axis=0
    )
    middle = (before + dot(mixed, proj[3]).astype(BF16).astype(F32)).astype(BF16).astype(F32)
    flat = normed(middle, gain_ref[1, 1:2, :])
    copies[1].wait()
    copies[2].wait()
    done = (middle + feed_forward(flat, w_in, w_out)).astype(BF16)
    low, high = done[:, :HALF], done[:, HALF:]
    keep_ref[...] = jnp.where(section == 0, low, high)
    send_ref[...] = jnp.where(section == 0, high, low)


def second_layer(above, x, below, left, right, gains, proj, w_in, w_out):
    tables = [jnp.asarray(t, BF16) for t in shifted_tables() + (ones_table(),)]
    return pl.pallas_call(
        second_kernel,
        out_shape=[jax.ShapeDtypeStruct((2 * TOKENS, HALF), BF16)] * 2,
        in_specs=[vmem()] * 13 + [hbm()] * 3,
        out_specs=[vmem()] * 2,
        scratch_shapes=[
            pltpu.VMEM((4, D, D), BF16),
            pltpu.VMEM((D, FF), BF16),
            pltpu.VMEM((FF, D), BF16),
            pltpu.SemaphoreType.DMA((3,)),
        ],
        compiler_params=pltpu.CompilerParams(vmem_limit_bytes=VMEM_LIMIT),
        name="second_layer",
    )(above, x, below, left, right, gains, *tables, proj, w_in, w_out)


def swap(value):
    return lax.ppermute(value, "section", [(0, 1), (1, 0)])


def device_number(section, lat, lon):
    return (section * lax.axis_size("lat") + lat) * lax.axis_size("lon") + lon


def move_rows(value, step):
    lats, lons = lax.axis_size("lat"), lax.axis_size("lon")
    pairs = []
    for place in range(2 * lats):
        target = place + step
        if 0 <= target < 2 * lats:
            for lon in range(lons):
                pairs.append(
                    (
                        device_number(place % 2, place // 2, lon),
                        device_number(target % 2, target // 2, lon),
                    )
                )
    return lax.ppermute(value, ALL_AXES, pairs)


def move_cols(value, step):
    lons = lax.axis_size("lon")
    return lax.ppermute(value, "lon", [(i, (i + step) % lons) for i in range(lons)])


def on_device(
    level_tokens, enc_query, enc_weights, attn_proj, expand, contract, gains,
):
    section = lax.axis_index("section")
    pieces = encode(level_tokens, enc_query, enc_weights)
    own = lax.all_to_all(
        pieces.reshape(64, CHUNK, 128), ("lat", "lon"), split_axis=0, concat_axis=0, tiled=True
    )
    other = swap(own)
    rows = 64 * CHUNK
    x = first_layer(
        own.reshape(rows, 128), other.reshape(rows, 128), enc_query, gains,
        enc_weights, attn_proj, expand, contract,
    )
    below = move_rows(x[:TOKENS], -1)
    above = move_rows(x[TOKENS:], 1)
    bands = (above, x[:TOKENS], x[TOKENS:], below)
    right = move_cols(jnp.concatenate([band[:QUAD] for band in bands], axis=0), -1)
    left = move_cols(jnp.concatenate([band[3 * QUAD :] for band in bands], axis=0), 1)
    keep, send = second_layer(above, x, below, left, right, gains, attn_proj, expand, contract)
    got = swap(send)
    top = jnp.where(section == 0, keep, got)
    bottom = jnp.where(section == 0, got, keep)
    return jnp.concatenate([top, bottom], axis=0).reshape(1, 8, 24, LATENTS, HALF)


def solution(mesh):
    return jax.shard_map(
        on_device,
        mesh=mesh,
        in_specs=(P(None, None, "lat", None, "lon", None, None), P(), P(), P(), P(), P(), P()),
        out_specs=P(None, "lat", "lon", None, "section"),
        check_vma=False,
    )
```

```python
import functools
import math

import jax
import jax.numpy as jnp
import numpy as np
from jax import lax
from jax.experimental import pallas as pl
from jax.experimental.pallas import tpu as pltpu
from jax.sharding import PartitionSpec as P

F32 = jnp.float32
BF16 = jnp.bfloat16
EPS = 1e-05
NEG = -1e30
HEADS = 16
HEAD = 32
GROUP = 8
LEVELS = 13
LATENTS = 3
D = 512
HALF = 256
FF = 2048
TOKENS = 144
CHUNK = 40
WIDE = 216
SCALE = math.log2(math.e) / math.sqrt(HEAD)
ALL_AXES = ("section", "lat", "lon")
VMEM_LIMIT = 24 * 1024 * 1024


def one_hot(rows, cols, pairs):
    out = np.zeros((rows, cols), np.float32)
    for row, col in pairs:
        out[row, col] = 1.0
    return out


def encoder_tables():
    expand = one_hot(
        128, LATENTS * HALF,
        [
            (l * GROUP + h, l * HALF + h * HEAD + e)
            for l in range(LATENTS) for h in range(GROUP) for e in range(HEAD)
        ],
    )
    scatter = [
        one_hot(
            8 * CHUNK, 72,
            [
                (b * CHUNK + half * 18 + d * 9 + w * 3 + l, l * 24 + w * 8 + (b + d * side) % 8)
                for b in range(8) for d in range(2) for w in range(3) for l in range(3)
            ],
        )
        for side in (1, -1) for half in range(2)
    ]
    return expand, np.stack(scatter)


def compact_table():
    tables = []
    for half in range(2):
        pairs = []
        for d in range(2):
            for r in range(4):
                for c in range(12):
                    for l in range(3):
                        token = ((c // 6) * 4 + r) * 18 + (c % 6) * 3 + l
                        row = half * 18 + d * 9 + (c % 3) * 3 + l
                        pairs.append((d * TOKENS + token, (r * 4 + c // 3) * CHUNK + row))
        tables.append(one_hot(2 * TOKENS, 16 * CHUNK, pairs))
    return np.stack(tables)


def band_tables():
    return np.stack([
        one_hot(WIDE, 2 * WIDE, [(cb * 36 + i, cb * 72 + rh * 36 + i) for cb in range(6) for i in range(36)])
        for rh in range(2)
    ])


def order_table():
    return one_hot(
        144, 160,
        [
            (r * 72 + l * 24 + cb * 6 + c, 4 + cb * 36 + r * 18 + c * 3 + l)
            for cb in range(4) for r in range(2) for c in range(6) for l in range(3)
        ],
    )


def dot(a, b):
    return jnp.dot(a, b, preferred_element_type=F32)


def pick(table, rows):
    return dot(table, rows).astype(BF16)


def normed_wide(values, gain):
    center = values - jnp.mean(values, -1, keepdims=True)
    spread = jnp.mean(center * center, -1, keepdims=True)
    return center * lax.rsqrt(spread + EPS) * gain


def normed(values, gain):
    return normed_wide(values, gain).astype(BF16)


def gelu(x):
    return 0.5 * x * (1.0 + lax.erf(x * (1.0 / math.sqrt(2.0))))


def by_head(block, heads=GROUP):
    lane = lax.broadcasted_iota(jnp.int32, (1, HALF), 1) // HEAD
    zero = jnp.zeros((), block.dtype)
    return jnp.concatenate([jnp.where(lane == h, block, zero) for h in range(heads)], axis=0)


def product_t(a, b):
    return lax.dot_general(a, b, (((1,), (1,)), ((), ())), preferred_element_type=F32)


def merge_heads(stack, count):
    lane = lax.broadcasted_iota(jnp.int32, (1, HALF), 1) // HEAD
    out = stack[:count]
    for h in range(1, GROUP):
        out = jnp.where(lane == h, stack[h * count : (h + 1) * count], out)
    return out


def attention_scores(q, k):
    return product_t(by_head(q).astype(BF16), k[:128]), product_t(q.astype(BF16), by_head(k[128:]))


def attention_weights(main, tail, bias):
    count = tail.shape[0]
    lane = lax.broadcasted_iota(jnp.int32, (1, 128), 1) // 16
    wide = lax.broadcasted_iota(jnp.int32, (1, HALF), 1) // HEAD
    if bias is not None:
        main = main + bias
    shift = jnp.zeros_like(tail)
    parts = []
    for h in range(GROUP):
        own = main[h * count : (h + 1) * count]
        top = jnp.max(
            jnp.maximum(own, jnp.where(lane == h, tail, -jnp.inf)), axis=-1, keepdims=True
        )
        parts.append(jnp.exp2(own - top))
        shift = jnp.where(lane == h, top, shift)
    rest = jnp.exp2(tail - shift)
    scale = jnp.zeros((count, HALF), F32)
    for h in range(GROUP):
        total = jnp.sum(parts[h] + jnp.where(lane == h, rest, 0.0), axis=-1, keepdims=True)
        scale = jnp.where(wide == h, total, scale)
    return jnp.concatenate(parts, axis=0).astype(BF16), rest.astype(BF16), scale


def attention_values(weights, rest, scale, v):
    total = merge_heads(dot(weights, v[:128]), scale.shape[0]) + dot(rest, by_head(v[128:]))
    return total / scale


def attend(windows, bias):
    groups = [slice(g * HALF, (g + 1) * HALF) for g in range(HEADS // GROUP)]
    jobs = [(q[:, g], k[:, g], v[:, g]) for q, k, v in windows for g in groups]
    scores, weights, outs = {}, {}, []
    for step in range(len(jobs) + 2):
        if step < len(jobs):
            scores[step] = attention_scores(*jobs[step][:2])
        if 1 <= step <= len(jobs):
            weights[step - 1] = attention_weights(*scores.pop(step - 1), bias)
        if step >= 2:
            outs.append(attention_values(*weights.pop(step - 2), jobs[step - 2][2]))
    return [
        jnp.concatenate(outs[i : i + len(groups)], axis=1)
        for i in range(0, len(outs), len(groups))
    ]


def windows_of(q, k, v, bounds):
    parts = [slice(w * TOKENS, (w + 1) * TOKENS) for w in range(len(bounds))]
    return [(q[a:b], k[part], v[part]) for (a, b), part in zip(bounds, parts)]


def feed_forward(tokens, w_in, w_out):
    total = None
    step = 512
    for i in range(FF // step):
        cols = slice(i * step, (i + 1) * step)
        hidden = gelu(dot(tokens, w_in[:, cols])).astype(BF16)
        part = dot(hidden, w_out[cols, :])
        total = part if total is None else total + part
    return total


def fetch(sources, targets, sems):
    return [
        pltpu.make_async_copy(source, target, sems.at[i])
        for i, (source, target) in enumerate(zip(sources, targets))
    ]


def encode_kernel(
    x_ref, query_ref, w_ref, expand_ref, scatter_ref, enc_hbm, in_hbm, out_hbm,
    out_ref, enc_next, in_next, out_next, keys, sems,
):
    side = lax.axis_index("lon") // 4
    copies = fetch(
        (enc_hbm.at[3], in_hbm.at[0], out_hbm.at[0]), (enc_next, in_next, out_next), sems
    )

    @pl.when(pl.program_id(0) == pl.num_programs(0) - 2)
    def _():
        for copy in copies:
            copy.start()

    @pl.when(pl.program_id(0) == 0)
    def _():
        query = jnp.concatenate([query_ref[...], jnp.zeros((5, D), BF16)], axis=0)
        latent = dot(query, w_ref[0]).astype(BF16).astype(F32)
        turned = latent.T
        col = lax.broadcasted_iota(jnp.int32, (HALF, 128), 1)
        head = lax.broadcasted_iota(jnp.int32, (HALF, 128), 0) // HEAD
        spread = jnp.zeros((HALF, 128), F32)
        for l in range(LATENTS):
            spread = jnp.where(col == l * GROUP + head, turned[:, l : l + 1], spread)
        keys[...] = (dot(w_ref[1], spread.astype(BF16)) * SCALE).astype(BF16)

    x = x_ref[...]
    rows = x.shape[0]
    count = rows // (LEVELS * 24)
    value = dot(x, w_ref[2])
    scores = dot(x, keys[...]).reshape(count * 3, LEVELS, 8, 128)
    expd = jnp.exp2(scores - jnp.max(scores, axis=1, keepdims=True))
    share = (expd / jnp.sum(expd, axis=1, keepdims=True)).reshape(rows, 128).astype(BF16)
    mixed = []
    for l in range(LATENTS):
        weighted = dot(share, expand_ref[:, l * HALF : (l + 1) * HALF]) * value
        mixed.append(jnp.sum(weighted.reshape(count * 3, LEVELS, 8, HALF), axis=1))
    for a in range(count):
        part = [m[3 * a : 3 * a + 3].reshape(24, HALF) for m in mixed]
        part = jnp.concatenate(part, axis=0).astype(BF16)
        out_ref[a * 8 * CHUNK : (a + 1) * 8 * CHUNK, :] = (
            dot(scatter_ref[2 * side], part[:, :128])
            + dot(scatter_ref[2 * side + 1], part[:, 128:])
        ).astype(BF16)

    @pl.when(pl.program_id(0) == pl.num_programs(0) - 1)
    def _():
        for copy in copies:
            copy.wait()


def vmem():
    return pl.BlockSpec(memory_space=pltpu.VMEM)


def hbm():
    return pl.BlockSpec(memory_space=pl.ANY)


def in_hbm_space(*arrays):
    return [pltpu.with_memory_space_constraint(a, pltpu.HBM) for a in arrays]


def encode(level_tokens, enc_query, enc_weights, expand, contract):
    source = level_tokens.transpose(0, 1, 2, 4, 5, 3, 6).reshape(-1, D)
    spread, scatter = encoder_tables()
    block = 2 * 24 * LEVELS
    steps = source.shape[0] // block
    return pl.pallas_call(
        encode_kernel,
        grid=(steps,),
        out_shape=[
            jax.ShapeDtypeStruct((steps * 16 * CHUNK, 128), BF16),
            pltpu.VMEM((D, D), BF16),
            pltpu.VMEM((D, FF), BF16),
            pltpu.VMEM((FF, D), BF16),
        ],
        in_specs=[
            pl.BlockSpec((block, D), lambda i: (i, 0)),
            pl.BlockSpec((LATENTS, D), lambda i: (0, 0)),
            pl.BlockSpec((3, D, HALF), lambda i: (0, 0, lax.axis_index("section"))),
            pl.BlockSpec(spread.shape, lambda i: (0, 0)),
            pl.BlockSpec(scatter.shape, lambda i: (0, 0, 0)),
        ] + [hbm()] * 3,
        out_specs=[pl.BlockSpec((16 * CHUNK, 128), lambda i: (i, 0))] + [hbm()] * 3,
        scratch_shapes=[pltpu.VMEM((D, 128), BF16), pltpu.SemaphoreType.DMA((3,))],
        compiler_params=pltpu.CompilerParams(vmem_limit_bytes=VMEM_LIMIT),
        name="encode_levels",
    )(
        *in_hbm_space(
            source, enc_query, enc_weights, jnp.asarray(spread, BF16), jnp.asarray(scatter, BF16),
            enc_weights, expand, contract,
        )
    )


def first_kernel(
    own_ref, other_ref, query_ref, gain_ref, compact_ref, bands_ref,
    proj_ref, enc_w, w_in, w_out, edge_ref, side_ref,
):
    proj = proj_ref.at[0]
    section = lax.axis_index("section")
    windows = []
    for group in range(2):
        parts = []
        for r in range(4):
            start = pl.multiple_of(((section * 4 + r) * 8 + group * 4) * CHUNK, 32)
            rows = pl.ds(start, 4 * CHUNK)
            parts.append(jnp.concatenate([own_ref[rows, :], other_ref[rows, :]], axis=1))
        block = jnp.concatenate(parts, axis=0)
        low, high = pick(compact_ref[0], block), pick(compact_ref[1], block)
        own = jnp.concatenate([low[:, :128], high[:, :128]], axis=1)
        other = jnp.concatenate([low[:, 128:], high[:, 128:]], axis=1)
        windows.append((own, other))
    own, other = [
        jnp.concatenate(
            [windows[1][i][TOKENS:], windows[0][i][:TOKENS], windows[1][i][:TOKENS], windows[0][i][TOKENS:]],
            axis=0,
        )
        for i in range(2)
    ]
    latent = lax.broadcasted_iota(jnp.int32, (4 * TOKENS, 1), 0) % LATENTS
    query = query_ref[...].astype(F32)
    base = jnp.where(
        latent == 0, query[0:1], jnp.where(latent == 1, query[1:2], query[2:3])
    )
    mine = pl.ds(pl.multiple_of(section * HALF, HALF), HALF)
    theirs = pl.ds(pl.multiple_of((1 - section) * HALF, HALF), HALF)
    tokens = base + dot(own, enc_w[mine, :]) + dot(other, enc_w[theirs, :])
    tokens = tokens.astype(BF16).astype(F32)
    wide = normed_wide(tokens, gain_ref[0, 0:1, :])
    flat = wide.astype(BF16)
    inner = slice(TOKENS // 2, 4 * TOKENS - TOKENS // 2)
    k = dot(flat, proj[1]).astype(BF16)
    v = dot(flat, proj[2]).astype(BF16)
    q = dot(wide[inner].astype(BF16), proj[0]) * SCALE
    bounds = ((0, 72), (72, 216), (216, 360), (360, 432))
    mixed = attend(windows_of(q, k, v, bounds), None)
    mixed = jnp.concatenate(mixed, axis=0).astype(BF16)
    middle = (tokens[inner] + dot(mixed, proj[3]).astype(BF16).astype(F32)).astype(BF16).astype(F32)
    flat = normed(middle, gain_ref[0, 1:2, :])
    done = (middle + feed_forward(flat, w_in, w_out)).astype(BF16)
    north, south = pick(bands_ref[0], done), pick(bands_ref[1], done)
    edge_ref[...] = jnp.where(section == 0, north, south)
    side_ref[...] = jnp.where(section == 0, south, north)


def first_layer(own, other, enc_query, gains, proj, weights):
    tables = [jnp.asarray(t, BF16) for t in (compact_table(), band_tables())]
    return pl.pallas_call(
        first_kernel,
        out_shape=[jax.ShapeDtypeStruct((WIDE, D), BF16)] * 2,
        in_specs=[vmem()] * 10,
        out_specs=[vmem()] * 2,
        compiler_params=pltpu.CompilerParams(vmem_limit_bytes=VMEM_LIMIT),
        name="first_layer",
    )(own, other, enc_query, gains, *tables, proj, *weights)


def side_kernel(
    halo_ref, own_ref, gain_ref, order_ref, proj_ref, in_hbm, out_hbm,
    keep_ref, send_ref, w_in, w_out, sems,
):
    copies = fetch((in_hbm.at[1], out_hbm.at[1]), (w_in, w_out), sems)
    second(
        False, copies, halo_ref, own_ref, gain_ref, order_ref, proj_ref.at[1], w_in, w_out,
        keep_ref, send_ref,
    )


def edge_kernel(
    halo_ref, own_ref, gain_ref, order_ref, proj_hbm, in_hbm, out_hbm,
    keep_ref, send_ref, w_in, w_out, proj, sems,
):
    copies = fetch(
        [proj_hbm.at[1, i] for i in (1, 2, 0, 3)] + [in_hbm.at[1], out_hbm.at[1]],
        [proj.at[i] for i in (1, 2, 0, 3)] + [w_in, w_out],
        sems,
    )
    second(
        True, copies, halo_ref, own_ref, gain_ref, order_ref, proj, w_in, w_out,
        keep_ref, send_ref,
    )


def second(
    at_edge, copies, halo_ref, own_ref, gain_ref, order_ref, proj, w_in, w_out,
    keep_ref, send_ref,
):
    for copy in copies:
        copy.start()
    section = lax.axis_index("section")
    gain = gain_ref[1, 0:1, :]
    halo = normed_wide(halo_ref[...].astype(F32), gain)
    own = normed_wide(own_ref[...].astype(F32), gain)
    keys = []
    for c in range(3):
        part = slice(72 * c, 72 * (c + 1))
        keys += [halo[part], own[part]]
    keys = jnp.concatenate(keys, axis=0).astype(BF16)
    for copy in copies[:-2]:
        copy.wait()
    q = dot(own[32:192].astype(BF16), proj[0]) * SCALE
    k = dot(keys, proj[1]).astype(BF16)
    v = dot(keys, proj[2]).astype(BF16)
    bias = None
    if at_edge:
        lat, last = lax.axis_index("lat"), lax.axis_size("lat") - 1
        pole = ((lat == 0) & (section == 0)) | ((lat == last) & (section == 1))
        outside = lax.broadcasted_iota(jnp.int32, (1, 128), 1) < TOKENS // 2
        bias = jnp.where(outside & pole, NEG, 0.0)
    mixed = attend(windows_of(q, k, v, ((0, 40), (40, 112), (112, 152))), bias)
    mixed.append(jnp.zeros((8, D), F32))
    mixed = pick(order_ref[...], jnp.concatenate(mixed, axis=0).astype(BF16))
    before = dot(order_ref[...], own_ref[32:192, :])
    middle = (before + dot(mixed, proj[3]).astype(BF16).astype(F32)).astype(BF16).astype(F32)
    flat = normed(middle, gain_ref[1, 1:2, :])
    for copy in copies[-2:]:
        copy.wait()
    done = (middle + feed_forward(flat, w_in, w_out)).astype(BF16)
    low, high = done[:, :HALF], done[:, HALF:]
    keep_ref[...] = jnp.where(section == 0, low, high)
    send_ref[...] = jnp.where(section == 0, high, low)


def second_layer(at_edge, halo, own, gains, order, proj, expand, contract):
    far = in_hbm_space(expand, contract)
    scratch = [pltpu.VMEM((D, FF), BF16), pltpu.VMEM((FF, D), BF16)]
    if at_edge:
        (proj,) = in_hbm_space(proj)
        scratch.append(pltpu.VMEM((4, D, D), BF16))
    return pl.pallas_call(
        edge_kernel if at_edge else side_kernel,
        out_shape=[jax.ShapeDtypeStruct((TOKENS, HALF), BF16)] * 2,
        in_specs=[vmem()] * 4 + [hbm() if at_edge else vmem()] + [hbm()] * 2,
        out_specs=[vmem()] * 2,
        scratch_shapes=scratch + [pltpu.SemaphoreType.DMA((6,))],
        compiler_params=pltpu.CompilerParams(vmem_limit_bytes=VMEM_LIMIT),
        name="second_layer_edge" if at_edge else "second_layer_side",
    )(halo, own, gains, order, proj, *far)


def swap(value):
    return lax.ppermute(value, "section", [(0, 1), (1, 0)])


def device_number(section, lat, lon):
    return (section * lax.axis_size("lat") + lat) * lax.axis_size("lon") + lon


def across(value):
    lats, lons = lax.axis_size("lat"), lax.axis_size("lon")
    pairs = []
    for lat in range(lats - 1):
        for lon in range(lons):
            south, north = device_number(1, lat, lon), device_number(0, lat + 1, lon)
            pairs += [(south, north), (north, south)]
    return lax.ppermute(value, ALL_AXES, pairs)


def on_device(
    level_tokens, enc_query, enc_weights, attn_proj, expand, contract, gains,
):
    section = lax.axis_index("section")
    pieces, *weights = encode(level_tokens, enc_query, enc_weights, expand, contract)
    own = lax.all_to_all(
        pieces.reshape(64, CHUNK, 128), ("lat", "lon"), split_axis=0, concat_axis=0, tiled=True
    )
    other = swap(own)
    rows = 64 * CHUNK
    edge, side = first_layer(
        own.reshape(rows, 128), other.reshape(rows, 128), enc_query, gains, attn_proj,
        weights,
    )
    far = across(edge)
    near = swap(side)
    order = jnp.asarray(order_table(), BF16)
    keep_side, send_side = second_layer(
        False, near, side, gains, order, attn_proj, expand, contract
    )
    got_side = swap(send_side)
    keep_edge, send_edge = second_layer(
        True, far, edge, gains, order, attn_proj, expand, contract
    )
    got_edge = swap(send_edge)
    first = section == 0
    out = jnp.concatenate(
        [
            jnp.where(first, keep_edge, got_edge),
            jnp.where(first, keep_side, got_side),
            jnp.where(first, got_side, keep_side),
            jnp.where(first, got_edge, keep_edge),
        ],
        axis=0,
    )
    return out.reshape(1, 8, LATENTS, 24, HALF).transpose(0, 1, 3, 2, 4)


def solution(mesh):
    return jax.shard_map(
        on_device,
        mesh=mesh,
        in_specs=(P(None, None, "lat", None, "lon", None, None), P(), P(), P(), P(), P(), P()),
        out_specs=P(None, "lat", "lon", None, "section"),
        check_vma=False,
    )
```

```python
import functools
import math

import jax
import jax.numpy as jnp
import numpy as np
from jax import lax
from jax.experimental import pallas as pl
from jax.experimental.pallas import tpu as pltpu
from jax.sharding import PartitionSpec as P

F32 = jnp.float32
BF16 = jnp.bfloat16
EPS = 1e-05
NEG = -1e30
HEADS = 16
HEAD = 32
GROUP = 8
LEVELS = 13
LATENTS = 3
D = 512
HALF = 256
FF = 2048
TOKENS = 144
CHUNK = 40
WIDE = 216
SCALE = math.log2(math.e) / math.sqrt(HEAD)
ALL_AXES = ("section", "lat", "lon")
VMEM_LIMIT = 24 * 1024 * 1024


def one_hot(rows, cols, pairs):
    out = np.zeros((rows, cols), np.float32)
    for row, col in pairs:
        out[row, col] = 1.0
    return out


def scatter_table():
    return np.stack([
        one_hot(
            8 * CHUNK, 144,
            [
                (
                    b * CHUNK + half * 18 + d * 9 + w * 3 + l,
                    half * 72 + l * 24 + w * 8 + (b + d * side) % 8,
                )
                for half in range(2)
                for b in range(8) for d in range(2) for w in range(3) for l in range(3)
            ],
        )
        for side in (1, -1)
    ])


def compact_table():
    tables = []
    for half in range(2):
        pairs = []
        for d in range(2):
            for r in range(4):
                for c in range(12):
                    for l in range(3):
                        token = ((c // 6) * 4 + r) * 18 + (c % 6) * 3 + l
                        row = half * 18 + d * 9 + (c % 3) * 3 + l
                        pairs.append((d * TOKENS + token, (r * 4 + c // 3) * CHUNK + row))
        tables.append(one_hot(2 * TOKENS, 16 * CHUNK, pairs))
    return np.stack(tables)


def band_tables():
    return np.stack([
        one_hot(WIDE, 2 * WIDE, [(cb * 36 + i, cb * 72 + rh * 36 + i) for cb in range(6) for i in range(36)])
        for rh in range(2)
    ])


def order_table():
    return one_hot(
        144, 160,
        [
            (r * 72 + l * 24 + cb * 6 + c, 4 + cb * 36 + r * 18 + c * 3 + l)
            for cb in range(4) for r in range(2) for c in range(6) for l in range(3)
        ],
    )


def dot(a, b):
    return jnp.dot(a, b, preferred_element_type=F32)


def pick(table, rows):
    return dot(table, rows).astype(BF16)


def normed_wide(values, gain):
    center = values - jnp.mean(values, -1, keepdims=True)
    spread = jnp.mean(center * center, -1, keepdims=True)
    return center * lax.rsqrt(spread + EPS) * gain


def normed(values, gain):
    return normed_wide(values, gain).astype(BF16)


def gelu(x):
    return 0.5 * x * (1.0 + lax.erf(x * (1.0 / math.sqrt(2.0))))


def by_head(block, heads=GROUP):
    lane = lax.broadcasted_iota(jnp.int32, (1, HALF), 1) // HEAD
    zero = jnp.zeros((), block.dtype)
    return jnp.concatenate([jnp.where(lane == h, block, zero) for h in range(heads)], axis=0)


def product_t(a, b):
    return lax.dot_general(a, b, (((1,), (1,)), ((), ())), preferred_element_type=F32)


def merge_heads(stack, count):
    lane = lax.broadcasted_iota(jnp.int32, (1, HALF), 1) // HEAD
    out = stack[:count]
    for h in range(1, GROUP):
        out = jnp.where(lane == h, stack[h * count : (h + 1) * count], out)
    return out


def attention_scores(q, k):
    return product_t(by_head(q).astype(BF16), k[:128]), product_t(q.astype(BF16), by_head(k[128:]))


def attention_weights(main, tail, bias):
    count = tail.shape[0]
    lane = lax.broadcasted_iota(jnp.int32, (1, 128), 1) // 16
    wide = lax.broadcasted_iota(jnp.int32, (1, HALF), 1) // HEAD
    if bias is not None:
        main = main + bias
    shift = jnp.zeros_like(tail)
    parts = []
    for h in range(GROUP):
        own = main[h * count : (h + 1) * count]
        top = jnp.max(
            jnp.maximum(own, jnp.where(lane == h, tail, -jnp.inf)), axis=-1, keepdims=True
        )
        parts.append(jnp.exp2(own - top))
        shift = jnp.where(lane == h, top, shift)
    rest = jnp.exp2(tail - shift)
    scale = jnp.zeros((count, HALF), F32)
    for h in range(GROUP):
        total = jnp.sum(parts[h] + jnp.where(lane == h, rest, 0.0), axis=-1, keepdims=True)
        scale = jnp.where(wide == h, total, scale)
    return jnp.concatenate(parts, axis=0).astype(BF16), rest.astype(BF16), scale


def attention_values(weights, rest, scale, v):
    total = merge_heads(dot(weights, v[:128]), scale.shape[0]) + dot(rest, by_head(v[128:]))
    return total / scale


def attend(windows, bias):
    groups = [slice(g * HALF, (g + 1) * HALF) for g in range(HEADS // GROUP)]
    jobs = [(q[:, g], k[:, g], v[:, g]) for q, k, v in windows for g in groups]
    scores, weights, outs = {}, {}, []
    for step in range(len(jobs) + 2):
        if step < len(jobs):
            scores[step] = attention_scores(*jobs[step][:2])
        if 1 <= step <= len(jobs):
            weights[step - 1] = attention_weights(*scores.pop(step - 1), bias)
        if step >= 2:
            outs.append(attention_values(*weights.pop(step - 2), jobs[step - 2][2]))
    return [
        jnp.concatenate(outs[i : i + len(groups)], axis=1)
        for i in range(0, len(outs), len(groups))
    ]


def windows_of(q, k, v, bounds):
    parts = [slice(w * TOKENS, (w + 1) * TOKENS) for w in range(len(bounds))]
    return [(q[a:b], k[part], v[part]) for (a, b), part in zip(bounds, parts)]


def feed_forward(tokens, w_in, w_out):
    total = None
    step = 512
    for i in range(FF // step):
        cols = slice(i * step, (i + 1) * step)
        hidden = gelu(dot(tokens, w_in[:, cols])).astype(BF16)
        part = dot(hidden, w_out[cols, :])
        total = part if total is None else total + part
    return total


def fetch(sources, targets, sems):
    return [
        pltpu.make_async_copy(source, target, sems.at[i])
        for i, (source, target) in enumerate(zip(sources, targets))
    ]


def encode_kernel(
    x_hbm, query_hbm, w_hbm, scatter_hbm, in_hbm, out_hbm,
    out_ref, enc_next, in_next, out_next, x, query, w, scatter, sems, next_sems,
):
    section = lax.axis_index("section")
    side = lax.axis_index("lon") // 4
    half = pl.ds(pl.multiple_of(section * HALF, HALF), HALF)
    steps = x.shape[0]
    rows = x.shape[1]
    count = rows // (LEVELS * 24)
    blocks = [x_hbm.at[pl.ds(i * rows, rows), :] for i in range(steps)]
    copies = fetch(
        [query_hbm] + [w_hbm.at[i, :, half] for i in range(3)]
        + [scatter_hbm.at[side]] + blocks,
        [query] + [w.at[i] for i in range(3)] + [scatter] + [x.at[i] for i in range(steps)],
        sems,
    )
    later = fetch(
        (w_hbm.at[3], in_hbm.at[0], out_hbm.at[0]), (enc_next, in_next, out_next), next_sems
    )
    for copy in copies:
        copy.start()
    for copy in copies[:3]:
        copy.wait()
    padded = jnp.concatenate([query[...], jnp.zeros((5, D), BF16)], axis=0)
    turned = dot(padded, w[0]).astype(BF16).astype(F32).T
    col = lax.broadcasted_iota(jnp.int32, (HALF, 128), 1)
    head = lax.broadcasted_iota(jnp.int32, (HALF, 128), 0) // HEAD
    spread = jnp.zeros((HALF, 128), F32)
    for l in range(LATENTS):
        spread = jnp.where(col == l * GROUP + head, turned[:, l : l + 1], spread)
    keys = (dot(w[1], spread.astype(BF16)) * SCALE).astype(BF16)
    row = lax.broadcasted_iota(jnp.int32, (128, HALF), 0)
    lane = lax.broadcasted_iota(jnp.int32, (128, HALF), 1) // HEAD
    expand = [
        jnp.where(row == l * GROUP + lane, 1.0, 0.0).astype(BF16) for l in range(LATENTS)
    ]
    for copy in copies[3:5]:
        copy.wait()
    for step in range(steps):
        copies[5 + step].wait()
        if step == 1:
            for copy in later:
                copy.start()
        block = x[step]
        value = dot(block, w[2])
        scores = dot(block, keys).reshape(count * 3, LEVELS, 8, 128)
        expd = jnp.exp2(scores - jnp.max(scores, axis=1, keepdims=True))
        share = (expd / jnp.sum(expd, axis=1, keepdims=True)).reshape(rows, 128).astype(BF16)
        mixed = []
        for l in range(LATENTS):
            weighted = dot(share, expand[l]) * value
            mixed.append(jnp.sum(weighted.reshape(count * 3, LEVELS, 8, HALF), axis=1))
        pairs = []
        for a in range(count):
            part = [m[3 * a : 3 * a + 3].reshape(24, HALF) for m in mixed]
            pairs.append(
                jnp.concatenate([p[:, :128] for p in part] + [p[:, 128:] for p in part], axis=0)
            )
        pieces = dot(scatter[...], jnp.concatenate(pairs, axis=1).astype(BF16)).astype(BF16)
        for a in range(count):
            start = (step * count + a) * 8 * CHUNK
            out_ref[start : start + 8 * CHUNK, :] = pieces[:, a * 128 : (a + 1) * 128]
    for copy in later:
        copy.wait()


def vmem():
    return pl.BlockSpec(memory_space=pltpu.VMEM)


def hbm():
    return pl.BlockSpec(memory_space=pl.ANY)


def in_hbm_space(*arrays):
    return [pltpu.with_memory_space_constraint(a, pltpu.HBM) for a in arrays]


def encode(level_tokens, enc_query, enc_weights, expand, contract):
    source = level_tokens.transpose(0, 1, 2, 4, 5, 3, 6).reshape(-1, D)
    scatter = scatter_table()
    block = 2 * 24 * LEVELS
    steps = source.shape[0] // block
    return pl.pallas_call(
        encode_kernel,
        out_shape=[
            jax.ShapeDtypeStruct((steps * 16 * CHUNK, 128), BF16),
            pltpu.VMEM((D, D), BF16),
            pltpu.VMEM((D, FF), BF16),
            pltpu.VMEM((FF, D), BF16),
        ],
        in_specs=[hbm()] * 6,
        out_specs=[vmem()] + [hbm()] * 3,
        scratch_shapes=[
            pltpu.VMEM((steps, block, D), BF16),
            pltpu.VMEM((LATENTS, D), BF16),
            pltpu.VMEM((3, D, HALF), BF16),
            pltpu.VMEM(scatter.shape[1:], BF16),
            pltpu.SemaphoreType.DMA((5 + steps,)),
            pltpu.SemaphoreType.DMA((3,)),
        ],
        compiler_params=pltpu.CompilerParams(vmem_limit_bytes=VMEM_LIMIT),
        name="encode_levels",
    )(
        *in_hbm_space(
            source, enc_query, enc_weights, jnp.asarray(scatter, BF16), expand, contract
        )
    )


def first_kernel(
    own_ref, other_ref, query_ref, gain_ref, compact_ref, bands_ref,
    proj_ref, enc_w, w_in, w_out, edge_ref, side_ref,
):
    proj = proj_ref.at[0]
    section = lax.axis_index("section")
    windows = []
    for group in range(2):
        parts = []
        for r in range(4):
            start = pl.multiple_of(((section * 4 + r) * 8 + group * 4) * CHUNK, 32)
            rows = pl.ds(start, 4 * CHUNK)
            parts.append(jnp.concatenate([own_ref[rows, :], other_ref[rows, :]], axis=1))
        block = jnp.concatenate(parts, axis=0)
        low, high = pick(compact_ref[0], block), pick(compact_ref[1], block)
        own = jnp.concatenate([low[:, :128], high[:, :128]], axis=1)
        other = jnp.concatenate([low[:, 128:], high[:, 128:]], axis=1)
        windows.append((own, other))
    own, other = [
        jnp.concatenate(
            [windows[1][i][TOKENS:], windows[0][i][:TOKENS], windows[1][i][:TOKENS], windows[0][i][TOKENS:]],
            axis=0,
        )
        for i in range(2)
    ]
    latent = lax.broadcasted_iota(jnp.int32, (4 * TOKENS, 1), 0) % LATENTS
    query = query_ref[...].astype(F32)
    base = jnp.where(
        latent == 0, query[0:1], jnp.where(latent == 1, query[1:2], query[2:3])
    )
    mine = pl.ds(pl.multiple_of(section * HALF, HALF), HALF)
    theirs = pl.ds(pl.multiple_of((1 - section) * HALF, HALF), HALF)
    tokens = base + dot(own, enc_w[mine, :]) + dot(other, enc_w[theirs, :])
    tokens = tokens.astype(BF16).astype(F32)
    wide = normed_wide(tokens, gain_ref[0, 0:1, :])
    flat = wide.astype(BF16)
    inner = slice(TOKENS // 2, 4 * TOKENS - TOKENS // 2)
    k = dot(flat, proj[1]).astype(BF16)
    v = dot(flat, proj[2]).astype(BF16)
    q = dot(wide[inner].astype(BF16), proj[0]) * SCALE
    bounds = ((0, 72), (72, 216), (216, 360), (360, 432))
    mixed = attend(windows_of(q, k, v, bounds), None)
    mixed = jnp.concatenate(mixed, axis=0).astype(BF16)
    middle = (tokens[inner] + dot(mixed, proj[3]).astype(BF16).astype(F32)).astype(BF16).astype(F32)
    flat = normed(middle, gain_ref[0, 1:2, :])
    done = (middle + feed_forward(flat, w_in, w_out)).astype(BF16)
    north, south = pick(bands_ref[0], done), pick(bands_ref[1], done)
    edge_ref[...] = jnp.where(section == 0, north, south)
    side_ref[...] = jnp.where(section == 0, south, north)


def first_layer(own, other, enc_query, gains, proj, weights):
    tables = [jnp.asarray(t, BF16) for t in (compact_table(), band_tables())]
    return pl.pallas_call(
        first_kernel,
        out_shape=[jax.ShapeDtypeStruct((WIDE, D), BF16)] * 2,
        in_specs=[vmem()] * 10,
        out_specs=[vmem()] * 2,
        compiler_params=pltpu.CompilerParams(vmem_limit_bytes=VMEM_LIMIT),
        name="first_layer",
    )(own, other, enc_query, gains, *tables, proj, *weights)


def side_kernel(
    halo_ref, own_ref, gain_ref, order_ref, proj_ref, in_hbm, out_hbm,
    keep_ref, send_ref, proj_next, w_in, w_out, sems,
):
    proj = proj_ref.at[1]
    copies = fetch((in_hbm.at[1], out_hbm.at[1], proj), (w_in, w_out, proj_next), sems)
    second(
        False, copies, halo_ref, own_ref, gain_ref, order_ref, proj, w_in, w_out,
        keep_ref, send_ref,
    )
    copies[2].wait()


def edge_kernel(
    halo_ref, own_ref, gain_ref, order_ref, proj, in_hbm, out_hbm,
    keep_ref, send_ref, w_in, w_out, sems,
):
    copies = fetch((in_hbm.at[1], out_hbm.at[1]), (w_in, w_out), sems)
    second(
        True, copies, halo_ref, own_ref, gain_ref, order_ref, proj, w_in, w_out,
        keep_ref, send_ref,
    )


def second(
    at_edge, copies, halo_ref, own_ref, gain_ref, order_ref, proj, w_in, w_out,
    keep_ref, send_ref,
):
    for copy in copies:
        copy.start()
    section = lax.axis_index("section")
    gain = gain_ref[1, 0:1, :]
    halo = normed_wide(halo_ref[...].astype(F32), gain)
    own = normed_wide(own_ref[...].astype(F32), gain)
    keys = []
    for c in range(3):
        part = slice(72 * c, 72 * (c + 1))
        keys += [halo[part], own[part]]
    keys = jnp.concatenate(keys, axis=0).astype(BF16)
    q = dot(own[32:192].astype(BF16), proj[0]) * SCALE
    k = dot(keys, proj[1]).astype(BF16)
    v = dot(keys, proj[2]).astype(BF16)
    bias = None
    if at_edge:
        lat, last = lax.axis_index("lat"), lax.axis_size("lat") - 1
        pole = ((lat == 0) & (section == 0)) | ((lat == last) & (section == 1))
        outside = lax.broadcasted_iota(jnp.int32, (1, 128), 1) < TOKENS // 2
        bias = jnp.where(outside & pole, NEG, 0.0)
    mixed = attend(windows_of(q, k, v, ((0, 40), (40, 112), (112, 152))), bias)
    mixed.append(jnp.zeros((8, D), F32))
    mixed = pick(order_ref[...], jnp.concatenate(mixed, axis=0).astype(BF16))
    before = dot(order_ref[...], own_ref[32:192, :])
    middle = (before + dot(mixed, proj[3]).astype(BF16).astype(F32)).astype(BF16).astype(F32)
    flat = normed(middle, gain_ref[1, 1:2, :])
    for copy in copies[:2]:
        copy.wait()
    done = (middle + feed_forward(flat, w_in, w_out)).astype(BF16)
    low, high = done[:, :HALF], done[:, HALF:]
    keep_ref[...] = jnp.where(section == 0, low, high)
    send_ref[...] = jnp.where(section == 0, high, low)


def second_layer(at_edge, halo, own, gains, order, proj, expand, contract):
    passed = [] if at_edge else [pltpu.VMEM(proj.shape[1:], BF16)]
    return pl.pallas_call(
        edge_kernel if at_edge else side_kernel,
        out_shape=[jax.ShapeDtypeStruct((TOKENS, HALF), BF16)] * 2 + passed,
        in_specs=[vmem()] * 5 + [hbm()] * 2,
        out_specs=[vmem()] * 2 + [hbm()] * len(passed),
        scratch_shapes=[
            pltpu.VMEM((D, FF), BF16),
            pltpu.VMEM((FF, D), BF16),
            pltpu.SemaphoreType.DMA((3,)),
        ],
        compiler_params=pltpu.CompilerParams(vmem_limit_bytes=VMEM_LIMIT),
        name="second_layer_edge" if at_edge else "second_layer_side",
    )(halo, own, gains, order, proj, *in_hbm_space(expand, contract))


def swap(value):
    return lax.ppermute(value, "section", [(0, 1), (1, 0)])


def device_number(section, lat, lon):
    return (section * lax.axis_size("lat") + lat) * lax.axis_size("lon") + lon


def across(value):
    lats, lons = lax.axis_size("lat"), lax.axis_size("lon")
    pairs = []
    for lat in range(lats - 1):
        for lon in range(lons):
            south, north = device_number(1, lat, lon), device_number(0, lat + 1, lon)
            pairs += [(south, north), (north, south)]
    return lax.ppermute(value, ALL_AXES, pairs)


def on_device(
    level_tokens, enc_query, enc_weights, attn_proj, expand, contract, gains,
):
    section = lax.axis_index("section")
    pieces, *weights = encode(level_tokens, enc_query, enc_weights, expand, contract)
    own = lax.all_to_all(
        pieces.reshape(64, CHUNK, 128), ("lat", "lon"), split_axis=0, concat_axis=0, tiled=True
    )
    other = swap(own)
    rows = 64 * CHUNK
    edge, side = first_layer(
        own.reshape(rows, 128), other.reshape(rows, 128), enc_query, gains, attn_proj,
        weights,
    )
    far = across(edge)
    near = swap(side)
    order = jnp.asarray(order_table(), BF16)
    keep_side, send_side, proj = second_layer(
        False, near, side, gains, order, attn_proj, expand, contract
    )
    got_side = swap(send_side)
    keep_edge, send_edge = second_layer(
        True, far, edge, gains, order, proj, expand, contract
    )
    got_edge = swap(send_edge)
    first = section == 0
    out = jnp.concatenate(
        [
            jnp.where(first, keep_edge, got_edge),
            jnp.where(first, keep_side, got_side),
            jnp.where(first, got_side, keep_side),
            jnp.where(first, got_edge, keep_edge),
        ],
        axis=0,
    )
    return out.reshape(1, 8, LATENTS, 24, HALF).transpose(0, 1, 3, 2, 4)


def solution(mesh):
    return jax.shard_map(
        on_device,
        mesh=mesh,
        in_specs=(P(None, None, "lat", None, "lon", None, None), P(), P(), P(), P(), P(), P()),
        out_specs=P(None, "lat", "lon", None, "section"),
        check_vma=False,
    )
```

```python
import functools
import math

import jax
import jax.numpy as jnp
import numpy as np
from jax import lax
from jax.experimental import pallas as pl
from jax.experimental.pallas import tpu as pltpu
from jax.sharding import PartitionSpec as P

F32 = jnp.float32
BF16 = jnp.bfloat16
EPS = 1e-05
NEG = -1e30
HEADS = 16
HEAD = 32
GROUP = 8
LEVELS = 13
LATENTS = 3
D = 512
HALF = 256
FF = 2048
TOKENS = 144
CHUNK = 40
WIDE = 216
SCALE = math.log2(math.e) / math.sqrt(HEAD)
ALL_AXES = ("section", "lat", "lon")
VMEM_LIMIT = 24 * 1024 * 1024


def one_hot(rows, cols, pairs):
    out = np.zeros((rows, cols), np.float32)
    for row, col in pairs:
        out[row, col] = 1.0
    return out


def scatter_table():
    return np.stack([
        one_hot(
            8 * CHUNK, 144,
            [
                (
                    b * CHUNK + half * 18 + d * 9 + w * 3 + l,
                    half * 72 + l * 24 + w * 8 + (b + d * side) % 8,
                )
                for half in range(2)
                for b in range(8) for d in range(2) for w in range(3) for l in range(3)
            ],
        )
        for side in (1, -1)
    ])


def compact_table():
    tables = []
    for half in range(2):
        pairs = []
        for d in range(2):
            for r in range(4):
                for c in range(12):
                    for l in range(3):
                        token = ((c // 6) * 4 + r) * 18 + (c % 6) * 3 + l
                        row = half * 18 + d * 9 + (c % 3) * 3 + l
                        pairs.append((d * TOKENS + token, (r * 4 + c // 3) * CHUNK + row))
        tables.append(one_hot(2 * TOKENS, 16 * CHUNK, pairs))
    return np.stack(tables)


def band_tables():
    return np.stack([
        one_hot(WIDE, 2 * WIDE, [(cb * 36 + i, cb * 72 + rh * 36 + i) for cb in range(6) for i in range(36)])
        for rh in range(2)
    ])


def order_table():
    return one_hot(
        144, 160,
        [
            (r * 72 + l * 24 + cb * 6 + c, 4 + cb * 36 + r * 18 + c * 3 + l)
            for cb in range(4) for r in range(2) for c in range(6) for l in range(3)
        ],
    )


def dot(a, b):
    return jnp.dot(a, b, preferred_element_type=F32)


def pick(table, rows):
    return dot(table, rows).astype(BF16)


def normed_wide(values, gain):
    center = values - jnp.mean(values, -1, keepdims=True)
    spread = jnp.mean(center * center, -1, keepdims=True)
    return center * lax.rsqrt(spread + EPS) * gain


def normed(values, gain):
    return normed_wide(values, gain).astype(BF16)


def gelu(x):
    return 0.5 * x * (1.0 + lax.erf(x * (1.0 / math.sqrt(2.0))))


def by_head(block, heads=GROUP):
    lane = lax.broadcasted_iota(jnp.int32, (1, HALF), 1) // HEAD
    zero = jnp.zeros((), block.dtype)
    return jnp.concatenate([jnp.where(lane == h, block, zero) for h in range(heads)], axis=0)


def product_t(a, b):
    return lax.dot_general(a, b, (((1,), (1,)), ((), ())), preferred_element_type=F32)


def merge_heads(stack, count):
    lane = lax.broadcasted_iota(jnp.int32, (1, HALF), 1) // HEAD
    out = stack[:count]
    for h in range(1, GROUP):
        out = jnp.where(lane == h, stack[h * count : (h + 1) * count], out)
    return out


def attention_scores(q, k):
    return product_t(by_head(q).astype(BF16), k[:128]), product_t(q.astype(BF16), by_head(k[128:]))


def attention_weights(main, tail, bias):
    count = tail.shape[0]
    lane = lax.broadcasted_iota(jnp.int32, (1, 128), 1) // 16
    wide = lax.broadcasted_iota(jnp.int32, (1, HALF), 1) // HEAD
    if bias is not None:
        main = main + bias
    shift = jnp.zeros_like(tail)
    parts = []
    for h in range(GROUP):
        own = main[h * count : (h + 1) * count]
        top = jnp.max(
            jnp.maximum(own, jnp.where(lane == h, tail, -jnp.inf)), axis=-1, keepdims=True
        )
        parts.append(jnp.exp2(own - top))
        shift = jnp.where(lane == h, top, shift)
    rest = jnp.exp2(tail - shift)
    scale = jnp.zeros((count, HALF), F32)
    for h in range(GROUP):
        total = jnp.sum(parts[h] + jnp.where(lane == h, rest, 0.0), axis=-1, keepdims=True)
        scale = jnp.where(wide == h, total, scale)
    return jnp.concatenate(parts, axis=0).astype(BF16), rest.astype(BF16), scale


def attention_values(weights, rest, scale, v):
    total = merge_heads(dot(weights, v[:128]), scale.shape[0]) + dot(rest, by_head(v[128:]))
    return total / scale


def attend(windows, bias):
    groups = [slice(g * HALF, (g + 1) * HALF) for g in range(HEADS // GROUP)]
    jobs = [(q[:, g], k[:, g], v[:, g]) for q, k, v in windows for g in groups]
    scores, weights, outs = {}, {}, []
    for step in range(len(jobs) + 2):
        if step < len(jobs):
            scores[step] = attention_scores(*jobs[step][:2])
        if 1 <= step <= len(jobs):
            weights[step - 1] = attention_weights(*scores.pop(step - 1), bias)
        if step >= 2:
            outs.append(attention_values(*weights.pop(step - 2), jobs[step - 2][2]))
    return [
        jnp.concatenate(outs[i : i + len(groups)], axis=1)
        for i in range(0, len(outs), len(groups))
    ]


def windows_of(q, k, v, bounds):
    parts = [slice(w * TOKENS, (w + 1) * TOKENS) for w in range(len(bounds))]
    return [(q[a:b], k[part], v[part]) for (a, b), part in zip(bounds, parts)]


def feed_forward(tokens, w_in, w_out):
    return dot(gelu(dot(tokens, w_in[...])).astype(BF16), w_out[...])


def fetch(sources, targets, sems):
    return [
        pltpu.make_async_copy(source, target, sems.at[i])
        for i, (source, target) in enumerate(zip(sources, targets))
    ]


def encode_kernel(
    x_hbm, query_hbm, w_hbm, scatter_hbm, in_hbm, out_hbm,
    out_ref, enc_next, in_next, out_next, x, query, w, scatter, sems, next_sems,
):
    section = lax.axis_index("section")
    side = lax.axis_index("lon") // 4
    half = pl.ds(pl.multiple_of(section * HALF, HALF), HALF)
    steps = x.shape[0]
    rows = x.shape[1]
    count = rows // (LEVELS * 24)
    blocks = [x_hbm.at[pl.ds(i * rows, rows), :] for i in range(steps)]
    copies = fetch(
        [query_hbm] + [w_hbm.at[i, :, half] for i in range(3)]
        + [scatter_hbm.at[side]] + blocks,
        [query] + [w.at[i] for i in range(3)] + [scatter] + [x.at[i] for i in range(steps)],
        sems,
    )
    later = fetch(
        (w_hbm.at[3], in_hbm.at[0], out_hbm.at[0]), (enc_next, in_next, out_next), next_sems
    )
    for copy in copies:
        copy.start()
    for copy in copies[:3]:
        copy.wait()
    padded = jnp.concatenate([query[...], jnp.zeros((5, D), BF16)], axis=0)
    turned = dot(padded, w[0]).astype(BF16).astype(F32).T
    col = lax.broadcasted_iota(jnp.int32, (HALF, 128), 1)
    head = lax.broadcasted_iota(jnp.int32, (HALF, 128), 0) // HEAD
    spread = jnp.zeros((HALF, 128), F32)
    for l in range(LATENTS):
        spread = jnp.where(col == l * GROUP + head, turned[:, l : l + 1], spread)
    keys = (dot(w[1], spread.astype(BF16)) * SCALE).astype(BF16)
    row = lax.broadcasted_iota(jnp.int32, (128, HALF), 0)
    lane = lax.broadcasted_iota(jnp.int32, (128, HALF), 1) // HEAD
    expand = [
        jnp.where(row == l * GROUP + lane, 1.0, 0.0).astype(BF16) for l in range(LATENTS)
    ]
    for copy in copies[3:5]:
        copy.wait()
    for step in range(steps):
        copies[5 + step].wait()
        if step == 1:
            for copy in later:
                copy.start()
        block = x[step]
        value = dot(block, w[2])
        scores = dot(block, keys).reshape(count * 3, LEVELS, 8, 128)
        expd = jnp.exp2(scores - jnp.max(scores, axis=1, keepdims=True))
        share = (expd / jnp.sum(expd, axis=1, keepdims=True)).reshape(rows, 128).astype(BF16)
        mixed = []
        for l in range(LATENTS):
            weighted = dot(share, expand[l]) * value
            mixed.append(jnp.sum(weighted.reshape(count * 3, LEVELS, 8, HALF), axis=1))
        pairs = []
        for a in range(count):
            part = [m[3 * a : 3 * a + 3].reshape(24, HALF) for m in mixed]
            pairs.append(
                jnp.concatenate([p[:, :128] for p in part] + [p[:, 128:] for p in part], axis=0)
            )
        pieces = dot(scatter[...], jnp.concatenate(pairs, axis=1).astype(BF16)).astype(BF16)
        for a in range(count):
            start = (step * count + a) * 8 * CHUNK
            out_ref[start : start + 8 * CHUNK, :] = pieces[:, a * 128 : (a + 1) * 128]
    for copy in later:
        copy.wait()


def vmem():
    return pl.BlockSpec(memory_space=pltpu.VMEM)


def hbm():
    return pl.BlockSpec(memory_space=pl.ANY)


def in_hbm_space(*arrays):
    return [pltpu.with_memory_space_constraint(a, pltpu.HBM) for a in arrays]


def encode(level_tokens, enc_query, enc_weights, expand, contract):
    source = level_tokens.transpose(0, 1, 2, 4, 5, 3, 6).reshape(-1, D)
    scatter = scatter_table()
    block = 2 * 24 * LEVELS
    steps = source.shape[0] // block
    return pl.pallas_call(
        encode_kernel,
        out_shape=[
            jax.ShapeDtypeStruct((steps * 16 * CHUNK, 128), BF16),
            pltpu.VMEM((D, D), BF16),
            pltpu.VMEM((D, FF), BF16),
            pltpu.VMEM((FF, D), BF16),
        ],
        in_specs=[hbm()] * 6,
        out_specs=[vmem()] + [hbm()] * 3,
        scratch_shapes=[
            pltpu.VMEM((steps, block, D), BF16),
            pltpu.VMEM((LATENTS, D), BF16),
            pltpu.VMEM((3, D, HALF), BF16),
            pltpu.VMEM(scatter.shape[1:], BF16),
            pltpu.SemaphoreType.DMA((5 + steps,)),
            pltpu.SemaphoreType.DMA((3,)),
        ],
        compiler_params=pltpu.CompilerParams(vmem_limit_bytes=VMEM_LIMIT),
        name="encode_levels",
    )(
        *in_hbm_space(
            source, enc_query, enc_weights, jnp.asarray(scatter, BF16), expand, contract
        )
    )


def first_kernel(
    own_ref, other_ref, query_ref, gain_ref, compact_ref, bands_ref,
    proj_ref, enc_w, w_in, w_out, edge_ref, side_ref,
):
    proj = proj_ref.at[0]
    section = lax.axis_index("section")
    windows = []
    for group in range(2):
        parts = []
        for r in range(4):
            start = pl.multiple_of(((section * 4 + r) * 8 + group * 4) * CHUNK, 32)
            rows = pl.ds(start, 4 * CHUNK)
            parts.append(jnp.concatenate([own_ref[rows, :], other_ref[rows, :]], axis=1))
        block = jnp.concatenate(parts, axis=0)
        low, high = pick(compact_ref[0], block), pick(compact_ref[1], block)
        own = jnp.concatenate([low[:, :128], high[:, :128]], axis=1)
        other = jnp.concatenate([low[:, 128:], high[:, 128:]], axis=1)
        windows.append((own, other))
    own, other = [
        jnp.concatenate(
            [windows[1][i][TOKENS:], windows[0][i][:TOKENS], windows[1][i][:TOKENS], windows[0][i][TOKENS:]],
            axis=0,
        )
        for i in range(2)
    ]
    latent = lax.broadcasted_iota(jnp.int32, (4 * TOKENS, 1), 0) % LATENTS
    query = query_ref[...].astype(F32)
    base = jnp.where(
        latent == 0, query[0:1], jnp.where(latent == 1, query[1:2], query[2:3])
    )
    mine = pl.ds(pl.multiple_of(section * HALF, HALF), HALF)
    theirs = pl.ds(pl.multiple_of((1 - section) * HALF, HALF), HALF)
    tokens = base + dot(own, enc_w[mine, :]) + dot(other, enc_w[theirs, :])
    tokens = tokens.astype(BF16).astype(F32)
    wide = normed_wide(tokens, gain_ref[0, 0:1, :])
    flat = wide.astype(BF16)
    inner = slice(TOKENS // 2, 4 * TOKENS - TOKENS // 2)
    k = dot(flat, proj[1]).astype(BF16)
    v = dot(flat, proj[2]).astype(BF16)
    q = dot(wide[inner].astype(BF16), proj[0]) * SCALE
    bounds = ((0, 72), (72, 216), (216, 360), (360, 432))
    mixed = attend(windows_of(q, k, v, bounds), None)
    mixed = jnp.concatenate(mixed, axis=0).astype(BF16)
    middle = (tokens[inner] + dot(mixed, proj[3]).astype(BF16).astype(F32)).astype(BF16).astype(F32)
    flat = normed(middle, gain_ref[0, 1:2, :])
    done = (middle + feed_forward(flat, w_in, w_out)).astype(BF16)
    north, south = pick(bands_ref[0], done), pick(bands_ref[1], done)
    edge_ref[...] = jnp.where(section == 0, north, south)
    side_ref[...] = jnp.where(section == 0, south, north)


def first_layer(own, other, enc_query, gains, proj, weights):
    tables = [jnp.asarray(t, BF16) for t in (compact_table(), band_tables())]
    return pl.pallas_call(
        first_kernel,
        out_shape=[jax.ShapeDtypeStruct((WIDE, D), BF16)] * 2,
        in_specs=[vmem()] * 10,
        out_specs=[vmem()] * 2,
        compiler_params=pltpu.CompilerParams(vmem_limit_bytes=VMEM_LIMIT),
        name="first_layer",
    )(own, other, enc_query, gains, *tables, proj, *weights)


def side_kernel(
    halo_ref, own_ref, gain_ref, order_ref, proj_ref, in_hbm, out_hbm,
    keep_ref, send_ref, proj_next, w_in, w_out, sems,
):
    proj = proj_ref.at[1]
    copies = fetch((in_hbm.at[1], out_hbm.at[1], proj), (w_in, w_out, proj_next), sems)
    second(
        False, copies, halo_ref, own_ref, gain_ref, order_ref, proj, w_in, w_out,
        keep_ref, send_ref,
    )
    copies[2].wait()


def edge_kernel(
    halo_ref, own_ref, gain_ref, order_ref, proj, in_hbm, out_hbm,
    keep_ref, send_ref, w_in, w_out, sems,
):
    copies = fetch((in_hbm.at[1], out_hbm.at[1]), (w_in, w_out), sems)
    second(
        True, copies, halo_ref, own_ref, gain_ref, order_ref, proj, w_in, w_out,
        keep_ref, send_ref,
    )


def second(
    at_edge, copies, halo_ref, own_ref, gain_ref, order_ref, proj, w_in, w_out,
    keep_ref, send_ref,
):
    for copy in copies:
        copy.start()
    section = lax.axis_index("section")
    gain = gain_ref[1, 0:1, :]
    halo = normed_wide(halo_ref[...].astype(F32), gain)
    own = normed_wide(own_ref[...].astype(F32), gain)
    keys = []
    for c in range(3):
        part = slice(72 * c, 72 * (c + 1))
        keys += [halo[part], own[part]]
    keys = jnp.concatenate(keys, axis=0).astype(BF16)
    q = dot(own[32:192].astype(BF16), proj[0]) * SCALE
    k = dot(keys, proj[1]).astype(BF16)
    v = dot(keys, proj[2]).astype(BF16)
    bias = None
    if at_edge:
        lat, last = lax.axis_index("lat"), lax.axis_size("lat") - 1
        pole = ((lat == 0) & (section == 0)) | ((lat == last) & (section == 1))
        outside = lax.broadcasted_iota(jnp.int32, (1, 128), 1) < TOKENS // 2
        bias = jnp.where(outside & pole, NEG, 0.0)
    mixed = attend(windows_of(q, k, v, ((0, 40), (40, 112), (112, 152))), bias)
    mixed.append(jnp.zeros((8, D), F32))
    mixed = pick(order_ref[...], jnp.concatenate(mixed, axis=0).astype(BF16))
    before = dot(order_ref[...], own_ref[32:192, :])
    middle = (before + dot(mixed, proj[3]).astype(BF16).astype(F32)).astype(BF16).astype(F32)
    flat = normed(middle, gain_ref[1, 1:2, :])
    for copy in copies[:2]:
        copy.wait()
    done = (middle + feed_forward(flat, w_in, w_out)).astype(BF16)
    low, high = done[:, :HALF], done[:, HALF:]
    keep_ref[...] = jnp.where(section == 0, low, high)
    send_ref[...] = jnp.where(section == 0, high, low)


def second_layer(at_edge, halo, own, gains, order, proj, expand, contract):
    passed = [] if at_edge else [pltpu.VMEM(proj.shape[1:], BF16)]
    return pl.pallas_call(
        edge_kernel if at_edge else side_kernel,
        out_shape=[jax.ShapeDtypeStruct((TOKENS, HALF), BF16)] * 2 + passed,
        in_specs=[vmem()] * 5 + [hbm()] * 2,
        out_specs=[vmem()] * 2 + [hbm()] * len(passed),
        scratch_shapes=[
            pltpu.VMEM((D, FF), BF16),
            pltpu.VMEM((FF, D), BF16),
            pltpu.SemaphoreType.DMA((3,)),
        ],
        compiler_params=pltpu.CompilerParams(vmem_limit_bytes=VMEM_LIMIT),
        name="second_layer_edge" if at_edge else "second_layer_side",
    )(halo, own, gains, order, proj, *in_hbm_space(expand, contract))


def swap(value):
    return lax.ppermute(value, "section", [(0, 1), (1, 0)])


def device_number(section, lat, lon):
    return (section * lax.axis_size("lat") + lat) * lax.axis_size("lon") + lon


def across(value):
    lats, lons = lax.axis_size("lat"), lax.axis_size("lon")
    pairs = []
    for lat in range(lats - 1):
        for lon in range(lons):
            south, north = device_number(1, lat, lon), device_number(0, lat + 1, lon)
            pairs += [(south, north), (north, south)]
    return lax.ppermute(value, ALL_AXES, pairs)


def on_device(
    level_tokens, enc_query, enc_weights, attn_proj, expand, contract, gains,
):
    section = lax.axis_index("section")
    pieces, *weights = encode(level_tokens, enc_query, enc_weights, expand, contract)
    own = lax.all_to_all(
        pieces.reshape(64, CHUNK, 128), ("lat", "lon"), split_axis=0, concat_axis=0, tiled=True
    )
    other = swap(own)
    rows = 64 * CHUNK
    edge, side = first_layer(
        own.reshape(rows, 128), other.reshape(rows, 128), enc_query, gains, attn_proj,
        weights,
    )
    far = across(edge)
    near = swap(side)
    order = jnp.asarray(order_table(), BF16)
    keep_side, send_side, proj = second_layer(
        False, near, side, gains, order, attn_proj, expand, contract
    )
    got_side = swap(send_side)
    keep_edge, send_edge = second_layer(
        True, far, edge, gains, order, proj, expand, contract
    )
    got_edge = swap(send_edge)
    first = section == 0
    ready = jnp.concatenate(
        [
            keep_edge,
            jnp.where(first, keep_side, got_side),
            jnp.where(first, got_side, keep_side),
            keep_edge,
        ],
        axis=0,
    )
    place = jnp.where(first, 3 * TOKENS, 0)
    out = lax.dynamic_update_slice(ready, got_edge, (place, 0))
    return out.reshape(1, 8, LATENTS, 24, HALF).transpose(0, 1, 3, 2, 4)


def solution(mesh):
    return jax.shard_map(
        on_device,
        mesh=mesh,
        in_specs=(P(None, None, "lat", None, "lon", None, None), P(), P(), P(), P(), P(), P()),
        out_specs=P(None, "lat", "lon", None, "section"),
        check_vma=False,
    )
```

```python
import functools
import math

import jax
import jax.numpy as jnp
import numpy as np
from jax import lax
from jax.experimental import pallas as pl
from jax.experimental.pallas import tpu as pltpu
from jax.sharding import PartitionSpec as P

F32 = jnp.float32
BF16 = jnp.bfloat16
EPS = 1e-05
NEG = -1e30
HEADS = 16
HEAD = 32
GROUP = 8
LEVELS = 13
LATENTS = 3
D = 512
HALF = 256
FF = 2048
TOKENS = 144
CHUNK = 40
WIDE = 216
SCALE = math.log2(math.e) / math.sqrt(HEAD)
ALL_AXES = ("section", "lat", "lon")
VMEM_LIMIT = 24 * 1024 * 1024


def one_hot(rows, cols, pairs):
    out = np.zeros((rows, cols), np.float32)
    for row, col in pairs:
        out[row, col] = 1.0
    return out


def scatter_table():
    return np.stack([
        one_hot(
            8 * CHUNK, 144,
            [
                (
                    b * CHUNK + half * 18 + d * 9 + w * 3 + l,
                    half * 72 + l * 24 + w * 8 + (b + d * side) % 8,
                )
                for half in range(2)
                for b in range(8) for d in range(2) for w in range(3) for l in range(3)
            ],
        )
        for side in (1, -1)
    ])


def compact_table():
    tables = []
    for half in range(2):
        pairs = []
        for d in range(2):
            for r in range(4):
                for c in range(12):
                    for l in range(3):
                        token = ((c // 6) * 4 + r) * 18 + (c % 6) * 3 + l
                        row = half * 18 + d * 9 + (c % 3) * 3 + l
                        pairs.append((d * TOKENS + token, (r * 4 + c // 3) * CHUNK + row))
        tables.append(one_hot(2 * TOKENS, 16 * CHUNK, pairs))
    return np.stack(tables)


def band_tables():
    return np.stack([
        one_hot(WIDE, 2 * WIDE, [(cb * 36 + i, cb * 72 + rh * 36 + i) for cb in range(6) for i in range(36)])
        for rh in range(2)
    ])


def order_table():
    return one_hot(
        144, 160,
        [
            (r * 72 + l * 24 + cb * 6 + c, 4 + cb * 36 + r * 18 + c * 3 + l)
            for cb in range(4) for r in range(2) for c in range(6) for l in range(3)
        ],
    )


def dot(a, b):
    return jnp.dot(a, b, preferred_element_type=F32)


def pick(table, rows):
    return dot(table, rows).astype(BF16)


def normed_wide(values, gain):
    center = values - jnp.mean(values, -1, keepdims=True)
    spread = jnp.mean(center * center, -1, keepdims=True)
    return center * lax.rsqrt(spread + EPS) * gain


def normed(values, gain):
    return normed_wide(values, gain).astype(BF16)


def gelu(x):
    return 0.5 * x * (1.0 + lax.erf(x * (1.0 / math.sqrt(2.0))))


def by_head(block, heads=GROUP):
    lane = lax.broadcasted_iota(jnp.int32, (1, HALF), 1) // HEAD
    zero = jnp.zeros((), block.dtype)
    return jnp.concatenate([jnp.where(lane == h, block, zero) for h in range(heads)], axis=0)


def product_t(a, b):
    return lax.dot_general(a, b, (((1,), (1,)), ((), ())), preferred_element_type=F32)


def merge_heads(stack, count):
    lane = lax.broadcasted_iota(jnp.int32, (1, HALF), 1) // HEAD
    out = stack[:count]
    for h in range(1, GROUP):
        out = jnp.where(lane == h, stack[h * count : (h + 1) * count], out)
    return out


def attention_scores(q, k):
    return product_t(by_head(q).astype(BF16), k[:128]), product_t(q.astype(BF16), by_head(k[128:]))


def attention_weights(main, tail, bias):
    count = tail.shape[0]
    lane = lax.broadcasted_iota(jnp.int32, (1, 128), 1) // 16
    wide = lax.broadcasted_iota(jnp.int32, (1, HALF), 1) // HEAD
    if bias is not None:
        main = main + bias
    shift = jnp.zeros_like(tail)
    parts = []
    for h in range(GROUP):
        own = main[h * count : (h + 1) * count]
        top = jnp.max(
            jnp.maximum(own, jnp.where(lane == h, tail, -jnp.inf)), axis=-1, keepdims=True
        )
        parts.append(jnp.exp2(own - top))
        shift = jnp.where(lane == h, top, shift)
    rest = jnp.exp2(tail - shift)
    scale = jnp.zeros((count, HALF), F32)
    for h in range(GROUP):
        total = jnp.sum(parts[h] + jnp.where(lane == h, rest, 0.0), axis=-1, keepdims=True)
        scale = jnp.where(wide == h, total, scale)
    return jnp.concatenate(parts, axis=0).astype(BF16), rest.astype(BF16), scale


def attention_values(weights, rest, scale, v):
    total = merge_heads(dot(weights, v[:128]), scale.shape[0]) + dot(rest, by_head(v[128:]))
    return total / scale


def attend(windows, bias):
    groups = [slice(g * HALF, (g + 1) * HALF) for g in range(HEADS // GROUP)]
    jobs = [(q[:, g], k[:, g], v[:, g]) for q, k, v in windows for g in groups]
    scores, weights, outs = {}, {}, []
    for step in range(len(jobs) + 2):
        if step < len(jobs):
            scores[step] = attention_scores(*jobs[step][:2])
        if 1 <= step <= len(jobs):
            weights[step - 1] = attention_weights(*scores.pop(step - 1), bias)
        if step >= 2:
            outs.append(attention_values(*weights.pop(step - 2), jobs[step - 2][2]))
    return [
        jnp.concatenate(outs[i : i + len(groups)], axis=1)
        for i in range(0, len(outs), len(groups))
    ]


def windows_of(q, k, v, bounds):
    parts = [slice(w * TOKENS, (w + 1) * TOKENS) for w in range(len(bounds))]
    return [(q[a:b], k[part], v[part]) for (a, b), part in zip(bounds, parts)]


def feed_forward(tokens, w_in, w_out):
    return dot(gelu(dot(tokens, w_in[...])).astype(BF16), w_out[...])


def fetch(sources, targets, sems):
    return [
        pltpu.make_async_copy(source, target, sems.at[i])
        for i, (source, target) in enumerate(zip(sources, targets))
    ]


def encode_kernel(
    x_hbm, query_hbm, w_hbm, scatter_hbm, in_hbm, out_hbm,
    out_ref, enc_next, in_next, out_next, x, query, w, scatter, sems, next_sems,
):
    section = lax.axis_index("section")
    side = lax.axis_index("lon") // 4
    half = pl.ds(pl.multiple_of(section * HALF, HALF), HALF)
    steps = x.shape[0]
    rows = x.shape[1]
    count = rows // (LEVELS * 24)
    blocks = [x_hbm.at[pl.ds(i * rows, rows), :] for i in range(steps)]
    copies = fetch(
        [query_hbm] + [w_hbm.at[i, :, half] for i in range(3)]
        + [scatter_hbm.at[side]] + blocks,
        [query] + [w.at[i] for i in range(3)] + [scatter] + [x.at[i] for i in range(steps)],
        sems,
    )
    later = fetch(
        (w_hbm.at[3], in_hbm.at[0], out_hbm.at[0]), (enc_next, in_next, out_next), next_sems
    )
    for copy in copies:
        copy.start()
    for copy in copies[:3]:
        copy.wait()
    padded = jnp.concatenate([query[...], jnp.zeros((5, D), BF16)], axis=0)
    turned = dot(padded, w[0]).astype(BF16).astype(F32).T
    col = lax.broadcasted_iota(jnp.int32, (HALF, 128), 1)
    head = lax.broadcasted_iota(jnp.int32, (HALF, 128), 0) // HEAD
    spread = jnp.zeros((HALF, 128), F32)
    for l in range(LATENTS):
        spread = jnp.where(col == l * GROUP + head, turned[:, l : l + 1], spread)
    keys = (dot(w[1], spread.astype(BF16)) * SCALE).astype(BF16)
    row = lax.broadcasted_iota(jnp.int32, (128, HALF), 0)
    lane = lax.broadcasted_iota(jnp.int32, (128, HALF), 1) // HEAD
    expand = [
        jnp.where(row == l * GROUP + lane, 1.0, 0.0).astype(BF16) for l in range(LATENTS)
    ]
    for copy in copies[3:]:
        copy.wait()
    for copy in later:
        copy.start()
    for step in range(steps):
        block = x[step]
        value = dot(block, w[2])
        scores = dot(block, keys).reshape(count * 3, LEVELS, 8, 128)
        expd = jnp.exp2(scores - jnp.max(scores, axis=1, keepdims=True))
        share = (expd / jnp.sum(expd, axis=1, keepdims=True)).reshape(rows, 128).astype(BF16)
        mixed = []
        for l in range(LATENTS):
            weighted = dot(share, expand[l]) * value
            mixed.append(jnp.sum(weighted.reshape(count * 3, LEVELS, 8, HALF), axis=1))
        pairs = []
        for a in range(count):
            part = [m[3 * a : 3 * a + 3].reshape(24, HALF) for m in mixed]
            pairs.append(
                jnp.concatenate([p[:, :128] for p in part] + [p[:, 128:] for p in part], axis=0)
            )
        pieces = dot(scatter[...], jnp.concatenate(pairs, axis=1).astype(BF16)).astype(BF16)
        for a in range(count):
            start = (step * count + a) * 8 * CHUNK
            out_ref[start : start + 8 * CHUNK, :] = pieces[:, a * 128 : (a + 1) * 128]
    for copy in later:
        copy.wait()


def vmem():
    return pl.BlockSpec(memory_space=pltpu.VMEM)


def hbm():
    return pl.BlockSpec(memory_space=pl.ANY)


def in_hbm_space(*arrays):
    return [pltpu.with_memory_space_constraint(a, pltpu.HBM) for a in arrays]


def encode(level_tokens, enc_query, enc_weights, expand, contract):
    source = level_tokens.transpose(0, 1, 2, 4, 5, 3, 6).reshape(-1, D)
    scatter = scatter_table()
    block = 8 * 24 * LEVELS
    steps = source.shape[0] // block
    return pl.pallas_call(
        encode_kernel,
        out_shape=[
            jax.ShapeDtypeStruct((steps * 64 * CHUNK, 128), BF16),
            pltpu.VMEM((D, D), BF16),
            pltpu.VMEM((D, FF), BF16),
            pltpu.VMEM((FF, D), BF16),
        ],
        in_specs=[hbm()] * 6,
        out_specs=[vmem()] + [hbm()] * 3,
        scratch_shapes=[
            pltpu.VMEM((steps, block, D), BF16),
            pltpu.VMEM((LATENTS, D), BF16),
            pltpu.VMEM((3, D, HALF), BF16),
            pltpu.VMEM(scatter.shape[1:], BF16),
            pltpu.SemaphoreType.DMA((5 + steps,)),
            pltpu.SemaphoreType.DMA((3,)),
        ],
        compiler_params=pltpu.CompilerParams(vmem_limit_bytes=VMEM_LIMIT),
        name="encode_levels",
    )(
        *in_hbm_space(
            source, enc_query, enc_weights, jnp.asarray(scatter, BF16), expand, contract
        )
    )


def first_kernel(
    own_ref, other_ref, query_ref, gain_ref, compact_ref, bands_ref,
    proj_ref, enc_w, w_in, w_out, edge_ref, side_ref,
):
    proj = proj_ref.at[0]
    section = lax.axis_index("section")
    windows = []
    for group in range(2):
        parts = []
        for r in range(4):
            start = pl.multiple_of(((section * 4 + r) * 8 + group * 4) * CHUNK, 32)
            rows = pl.ds(start, 4 * CHUNK)
            parts.append(jnp.concatenate([own_ref[rows, :], other_ref[rows, :]], axis=1))
        block = jnp.concatenate(parts, axis=0)
        low, high = pick(compact_ref[0], block), pick(compact_ref[1], block)
        own = jnp.concatenate([low[:, :128], high[:, :128]], axis=1)
        other = jnp.concatenate([low[:, 128:], high[:, 128:]], axis=1)
        windows.append((own, other))
    own, other = [
        jnp.concatenate(
            [windows[1][i][TOKENS:], windows[0][i][:TOKENS], windows[1][i][:TOKENS], windows[0][i][TOKENS:]],
            axis=0,
        )
        for i in range(2)
    ]
    latent = lax.broadcasted_iota(jnp.int32, (4 * TOKENS, 1), 0) % LATENTS
    query = query_ref[...].astype(F32)
    base = jnp.where(
        latent == 0, query[0:1], jnp.where(latent == 1, query[1:2], query[2:3])
    )
    mine = pl.ds(pl.multiple_of(section * HALF, HALF), HALF)
    theirs = pl.ds(pl.multiple_of((1 - section) * HALF, HALF), HALF)
    tokens = base + dot(own, enc_w[mine, :]) + dot(other, enc_w[theirs, :])
    tokens = tokens.astype(BF16).astype(F32)
    wide = normed_wide(tokens, gain_ref[0, 0:1, :])
    flat = wide.astype(BF16)
    inner = slice(TOKENS // 2, 4 * TOKENS - TOKENS // 2)
    k = dot(flat, proj[1]).astype(BF16)
    v = dot(flat, proj[2]).astype(BF16)
    q = dot(wide[inner].astype(BF16), proj[0]) * SCALE
    bounds = ((0, 72), (72, 216), (216, 360), (360, 432))
    mixed = attend(windows_of(q, k, v, bounds), None)
    mixed = jnp.concatenate(mixed, axis=0).astype(BF16)
    middle = (tokens[inner] + dot(mixed, proj[3]).astype(BF16).astype(F32)).astype(BF16).astype(F32)
    flat = normed(middle, gain_ref[0, 1:2, :])
    done = (middle + feed_forward(flat, w_in, w_out)).astype(BF16)
    north, south = pick(bands_ref[0], done), pick(bands_ref[1], done)
    edge_ref[...] = jnp.where(section == 0, north, south)
    side_ref[...] = jnp.where(section == 0, south, north)


def first_layer(own, other, enc_query, gains, proj, weights):
    tables = [jnp.asarray(t, BF16) for t in (compact_table(), band_tables())]
    return pl.pallas_call(
        first_kernel,
        out_shape=[jax.ShapeDtypeStruct((WIDE, D), BF16)] * 2,
        in_specs=[vmem()] * 10,
        out_specs=[vmem()] * 2,
        compiler_params=pltpu.CompilerParams(vmem_limit_bytes=VMEM_LIMIT),
        name="first_layer",
    )(own, other, enc_query, gains, *tables, proj, *weights)


def side_kernel(
    halo_ref, own_ref, gain_ref, order_ref, proj_ref, in_hbm, out_hbm,
    keep_ref, send_ref, proj_next, w_in, w_out, sems,
):
    proj = proj_ref.at[1]
    copies = fetch((in_hbm.at[1], out_hbm.at[1], proj), (w_in, w_out, proj_next), sems)
    second(
        False, copies, halo_ref, own_ref, gain_ref, order_ref, proj, w_in, w_out,
        keep_ref, send_ref,
    )
    copies[2].wait()


def edge_kernel(
    halo_ref, own_ref, gain_ref, order_ref, proj, in_hbm, out_hbm,
    keep_ref, send_ref, w_in, w_out, sems,
):
    copies = fetch((in_hbm.at[1], out_hbm.at[1]), (w_in, w_out), sems)
    second(
        True, copies, halo_ref, own_ref, gain_ref, order_ref, proj, w_in, w_out,
        keep_ref, send_ref,
    )


def second(
    at_edge, copies, halo_ref, own_ref, gain_ref, order_ref, proj, w_in, w_out,
    keep_ref, send_ref,
):
    for copy in copies:
        copy.start()
    section = lax.axis_index("section")
    gain = gain_ref[1, 0:1, :]
    halo = normed_wide(halo_ref[...].astype(F32), gain)
    own = normed_wide(own_ref[...].astype(F32), gain)
    keys = []
    for c in range(3):
        part = slice(72 * c, 72 * (c + 1))
        keys += [halo[part], own[part]]
    keys = jnp.concatenate(keys, axis=0).astype(BF16)
    q = dot(own[32:192].astype(BF16), proj[0]) * SCALE
    k = dot(keys, proj[1]).astype(BF16)
    v = dot(keys, proj[2]).astype(BF16)
    bias = None
    if at_edge:
        lat, last = lax.axis_index("lat"), lax.axis_size("lat") - 1
        pole = ((lat == 0) & (section == 0)) | ((lat == last) & (section == 1))
        outside = lax.broadcasted_iota(jnp.int32, (1, 128), 1) < TOKENS // 2
        bias = jnp.where(outside & pole, NEG, 0.0)
    mixed = attend(windows_of(q, k, v, ((0, 40), (40, 112), (112, 152))), bias)
    mixed.append(jnp.zeros((8, D), F32))
    mixed = pick(order_ref[...], jnp.concatenate(mixed, axis=0).astype(BF16))
    before = dot(order_ref[...], own_ref[32:192, :])
    middle = (before + dot(mixed, proj[3]).astype(BF16).astype(F32)).astype(BF16).astype(F32)
    flat = normed(middle, gain_ref[1, 1:2, :])
    for copy in copies[:2]:
        copy.wait()
    done = (middle + feed_forward(flat, w_in, w_out)).astype(BF16)
    low, high = done[:, :HALF], done[:, HALF:]
    keep_ref[...] = jnp.where(section == 0, low, high)
    send_ref[...] = jnp.where(section == 0, high, low)


def second_layer(at_edge, halo, own, gains, order, proj, expand, contract):
    passed = [] if at_edge else [pltpu.VMEM(proj.shape[1:], BF16)]
    return pl.pallas_call(
        edge_kernel if at_edge else side_kernel,
        out_shape=[jax.ShapeDtypeStruct((TOKENS, HALF), BF16)] * 2 + passed,
        in_specs=[vmem()] * 5 + [hbm()] * 2,
        out_specs=[vmem()] * 2 + [hbm()] * len(passed),
        scratch_shapes=[
            pltpu.VMEM((D, FF), BF16),
            pltpu.VMEM((FF, D), BF16),
            pltpu.SemaphoreType.DMA((3,)),
        ],
        compiler_params=pltpu.CompilerParams(vmem_limit_bytes=VMEM_LIMIT),
        name="second_layer_edge" if at_edge else "second_layer_side",
    )(halo, own, gains, order, proj, *in_hbm_space(expand, contract))


def swap(value):
    return lax.ppermute(value, "section", [(0, 1), (1, 0)])


def device_number(section, lat, lon):
    return (section * lax.axis_size("lat") + lat) * lax.axis_size("lon") + lon


def across(value):
    lats, lons = lax.axis_size("lat"), lax.axis_size("lon")
    pairs = []
    for lat in range(lats - 1):
        for lon in range(lons):
            south, north = device_number(1, lat, lon), device_number(0, lat + 1, lon)
            pairs += [(south, north), (north, south)]
    return lax.ppermute(value, ALL_AXES, pairs)


def on_device(
    level_tokens, enc_query, enc_weights, attn_proj, expand, contract, gains,
):
    section = lax.axis_index("section")
    pieces, *weights = encode(level_tokens, enc_query, enc_weights, expand, contract)
    own = lax.all_to_all(
        pieces.reshape(64, CHUNK, 128), ("lat", "lon"), split_axis=0, concat_axis=0, tiled=True
    )
    other = swap(own)
    rows = 64 * CHUNK
    edge, side = first_layer(
        own.reshape(rows, 128), other.reshape(rows, 128), enc_query, gains, attn_proj,
        weights,
    )
    far = across(edge)
    near = swap(side)
    order = jnp.asarray(order_table(), BF16)
    keep_side, send_side, proj = second_layer(
        False, near, side, gains, order, attn_proj, expand, contract
    )
    got_side = swap(send_side)
    keep_edge, send_edge = second_layer(
        True, far, edge, gains, order, proj, expand, contract
    )
    got_edge = swap(send_edge)
    first = section == 0
    ready = jnp.concatenate(
        [
            keep_edge,
            jnp.where(first, keep_side, got_side),
            jnp.where(first, got_side, keep_side),
            keep_edge,
        ],
        axis=0,
    )
    place = jnp.where(first, 3 * TOKENS, 0)
    out = lax.dynamic_update_slice(ready, got_edge, (place, 0))
    return out.reshape(1, 8, LATENTS, 24, HALF).transpose(0, 1, 3, 2, 4)


def solution(mesh):
    return jax.shard_map(
        on_device,
        mesh=mesh,
        in_specs=(P(None, None, "lat", None, "lon", None, None), P(), P(), P(), P(), P(), P()),
        out_specs=P(None, "lat", "lon", None, "section"),
        check_vma=False,
    )
```
